32 devices in a mesh: section: 2 (over x), expert: 16 (over z, y, core).
Axes of the slice: x: 2, y: 2, z: 4, core: 2. Of those that a mesh axis runs over, the one named last changes fastest.
Arguments:
- entering: bfloat16 [2, 512, 3584], P('section', 'expert'), may hold values from -6 to 6
- saved: bfloat16 [2, 16, 384, 384], P('section', 'expert'), may hold values from -6 to 6
- routes: int32 [2, 2, 512, 1], P(None, 'section', 'expert'), may hold values from 0 to 1; in each aligned block of 32 rows (0 to 31, 32 to 63, ..., all dimensions but the last counted through in order) at most 24 rows name the same one
- gates: float32 [2, 2, 512, 1], P(None, 'section', 'expert'), may hold values from 0.1 to 1
- w_in: bfloat16 [2, 16, 3584, 384], P('section', 'expert'), may hold values from -0.09375 to 0.09375
- w_out: bfloat16 [2, 16, 192, 3584], P('section', 'expert'), may hold values from -0.15625 to 0.15625
Outputs:
- results: bfloat16 [2, 2, 512, 3584], P(None, 'section', 'expert')
The draws below stay inside these ranges and needn't reach their ends.
Inputs may be any that keep to these rules, and one draw needn't show every extreme that they name: `routes`: each row names one expert; in the rows of one device for one tick and layer no expert is named more than 24 times.
All inputs are finite; a program needn't handle non-finite values.
Results may differ from the reference program's by a relative error of at most 0.015.
Values may be sent and summed in bfloat16 or wider, within the bound.
A program may use at most 64 MiB of HBM per device.

```python
import math
import jax
import jax.numpy as jnp
import numpy as np
from jax import lax

D = 3584
F = 1536
SHARDS = 8
TOP = 1
TOK_DEV = 32
SECTIONS = 2
EXPERTS = 2
HDEV = 192
TOKENS = 512
CAP = 24
N_EXPERT = 16


def block_levels(key, extent, pieces, smallest, top_value):
    gain, own = 1.0, jax.random.fold_in(key, 6)
    for position, parts in pieces:
        steps = jnp.exp(jax.random.uniform(jax.random.fold_in(own, position), (parts,), jnp.float32, smallest / len(pieces), top_value / len(pieces)))
        gain = gain * jnp.repeat(steps, extent[position] // parts).reshape([-1 if axis == position else 1 for axis in range(len(extent))])
    return gain


def assign_block(rng, own, number, rows, count, top, bound, slope):
    ranking = jax.random.permutation(rng, count)
    crowded, ordinary = load_shares(count, rows * top, bound, slope, True), load_shares(count, rows * top, bound, slope, False)
    places = jnp.arange(count)

    def named(lengths, offset_by):
        used = int((lengths > 0).sum())
        fixed = max(1, used // 4)
        moved = fixed + (places - fixed + offset_by * (used - fixed)) % max(1, count - fixed)
        return jnp.zeros((count,), jnp.int32).at[ranking[jnp.where(places < fixed, places, moved)]].set(jnp.asarray(lengths, jnp.int32))

    lengths = jnp.where(number % 4 == 0, named(crowded, number // 4), named(ordinary, number - number // 4 - 1))
    mixed = jax.random.permutation(jax.random.fold_in(own, 3), count)
    donor, sink = mixed[0:count // 2 * 2:2], mixed[1:count // 2 * 2:2]
    slack = jnp.minimum(lengths[donor] - 1, bound - lengths[sink]) // 2
    slack = jnp.where((donor == ranking[0]) | (sink == ranking[0]) | (lengths[sink] == 0), 0, jnp.maximum(slack, 0))
    moved = jax.random.randint(jax.random.fold_in(own, 4), (count // 2,), 0, 1 << 20) % (slack + 1)
    lengths = lengths.at[donor].add(-moved).at[sink].add(moved)
    members = jnp.searchsorted(jnp.cumsum(lengths), jnp.arange(rows * top), side="right").astype(jnp.int32)
    table = members.reshape(top, rows).T
    table = table[jax.random.permutation(jax.random.fold_in(own, 1), rows)]
    offset_by = jax.random.randint(jax.random.fold_in(own, 2), (rows, 1), 0, top)
    return jnp.take_along_axis(table, (jnp.arange(top)[None, :] + offset_by) % top, axis=1)


def load_shares(amount, total, limit, slope, full):
    loads = [(1 << 20) // math.isqrt(grade ** slope) + 1 for grade in range(1, amount + 1)]
    largest = limit if full else min(limit, max(-(-total // amount), total * loads[0] // sum(loads)))
    least = 1 if total - largest >= amount - 1 else 0
    holding, spare = [largest] + [least] * (amount - 1), total - largest - least * (amount - 1)
    while spare > 0:
        movable = [i for i in range(1, amount) if holding[i] < largest] or [i for i in range(1, amount) if holding[i] < limit]
        whole, remaining = sum([loads[i] for i in movable]), spare
        for i in movable:
            extra = min(limit - holding[i], max(1, remaining * loads[i] // whole), spare)
            holding[i] = holding[i] + extra
            spare = spare - extra
    return np.array(holding)


def centred(rng, dims, spread, most, pieces=(), held_as=jnp.bfloat16):
    result = jax.random.normal(rng, dims, jnp.float32) * spread
    if len(pieces) > 0:
        result = block_levels(rng, dims, pieces, -0.22, 0.18) * result
    return jnp.clip(result, min=-most, max=most).astype(held_as)


def setup_inputs(seed: int = 0) -> dict:
    key_of = jax.random.split(jax.random.key(seed), 7)
    entering = centred(key_of[0], (SECTIONS, TOKENS, D), 1.0, 6.0, ((0, 2), (1, 16)))
    saved = centred(key_of[1], (SECTIONS, N_EXPERT, N_EXPERT * CAP, 2 * HDEV), 1.0, 6.0, ((0, 2), (1, 16)))
    routes_keys = jax.random.split(jax.random.fold_in(key_of[2], 1), 2 * SECTIONS * TOKENS // TOK_DEV)
    routes_turns = jax.random.permutation(jax.random.fold_in(key_of[2], 3), 2 * SECTIONS * TOKENS // TOK_DEV)
    routes = jax.vmap(lambda own, number: assign_block(jax.random.fold_in(key_of[2], 2), own, number, TOK_DEV, EXPERTS, TOP, CAP, 2))(routes_keys, routes_turns).reshape((2, SECTIONS, TOKENS, TOP))
    gates = jnp.clip(0.1 + 0.9 * jax.random.uniform(key_of[3], (2, SECTIONS, TOKENS, TOP), jnp.float32) ** block_levels(key_of[3], (2, SECTIONS, TOKENS, TOP), ((1, 2), (2, 16)), -0.2, 0.2), 0.1, 1.0)
    w_in = centred(key_of[4], (SECTIONS, N_EXPERT, D, 2 * HDEV), D ** -0.5, 0.09375, ((0, 2), (1, 16)))
    w_out = centred(key_of[5], (SECTIONS, N_EXPERT, HDEV, D), F ** -0.5, 0.15625, ((0, 2), (1, 16)))
    return {"entering": entering, "saved": saved, "routes": routes, "gates": gates, "w_in": w_in, "w_out": w_out}


def silu_slope(gate_vals):
    sigmoid_vals = jax.nn.sigmoid(gate_vals)
    return sigmoid_vals * (1.0 + gate_vals * (1.0 - sigmoid_vals))


def slot_rows(routes):
    per_block = routes.reshape(N_EXPERT, TOK_DEV * TOP)
    expert_ids = jnp.arange(EXPERTS, dtype=jnp.int32)
    onehot = (per_block[:, :, None] == expert_ids[None, None, :]).astype(jnp.int32)
    before = (jnp.cumsum(onehot, axis=1) - onehot).astype(jnp.int32)
    slot_ids = jnp.sum(before * onehot, axis=2).astype(jnp.int32)
    block_ids = jnp.arange(N_EXPERT, dtype=jnp.int32)[:, None]
    return (block_ids * CAP + slot_ids).astype(jnp.int32).reshape(TOKENS, TOP)


def place_rows(data, routes, rows_at):
    buffer = jnp.zeros((EXPERTS, N_EXPERT * CAP, D), data.dtype)
    source = jnp.broadcast_to(data[:, None, :], (TOKENS, TOP, D))
    return buffer.at[routes, rows_at].set(source)


def expert_forward(packed):
    token_rows, w_in_e, w_out_e = packed
    pre_act = jnp.einsum("rd,jdh->jrh", token_rows.astype(jnp.float32), w_in_e.astype(jnp.float32))
    gate_vals = pre_act[..., :HDEV]
    up_vals = pre_act[..., HDEV:]
    hidden = (jax.nn.silu(gate_vals) * up_vals).astype(jnp.bfloat16)
    slice_part = jnp.einsum("jrh,jhd->jrd", hidden.astype(jnp.float32), w_out_e.astype(jnp.float32)).astype(jnp.bfloat16)
    return jnp.sum(slice_part.astype(jnp.float32), axis=0)


def expert_backward(packed):
    grad_rows, saved_e, w_in_e, w_out_e = packed
    gate_vals = saved_e[..., :HDEV].astype(jnp.float32)
    up_vals = saved_e[..., HDEV:].astype(jnp.float32)
    d_hidden = jnp.einsum("rd,jhd->jrh", grad_rows.astype(jnp.float32), w_out_e.astype(jnp.float32))
    d_gate = d_hidden * up_vals * silu_slope(gate_vals)
    d_up = d_hidden * jax.nn.silu(gate_vals)
    d_pre = jnp.concatenate([d_gate, d_up], axis=-1).astype(jnp.bfloat16)
    slice_back = jnp.einsum("jrh,jdh->jrd", d_pre.astype(jnp.float32), w_in_e.astype(jnp.float32)).astype(jnp.bfloat16)
    return jnp.sum(slice_back.astype(jnp.float32), axis=0)


def combine_rows(inputs, outputs, routes, rows_at, weights):
    picked = outputs[routes, rows_at]
    mixed_sum = jnp.sum(weights[:, :, None] * picked, axis=1)
    return (inputs.astype(jnp.float32) + mixed_sum).astype(jnp.bfloat16)


def forward_map(packed):
    inputs, routes, weights, w_in_s, w_out_s = packed
    rows_at = slot_rows(routes)
    buffer = place_rows(inputs, routes, rows_at)
    w_in_g = w_in_s.reshape(EXPERTS, SHARDS, D, 2 * HDEV)
    w_out_g = w_out_s.reshape(EXPERTS, SHARDS, HDEV, D)
    outputs = lax.map(expert_forward, (buffer, w_in_g, w_out_g))
    return combine_rows(inputs, outputs, routes, rows_at, weights)


def backward_map(packed):
    grad_in, saved_s, routes, weights, w_in_s, w_out_s = packed
    rows_at = slot_rows(routes)
    buffer = place_rows(grad_in, routes, rows_at)
    saved_groups = saved_s.reshape(EXPERTS, SHARDS, N_EXPERT * CAP, 2 * HDEV)
    w_in_g = w_in_s.reshape(EXPERTS, SHARDS, D, 2 * HDEV)
    w_out_g = w_out_s.reshape(EXPERTS, SHARDS, HDEV, D)
    outputs = lax.map(expert_backward, (buffer, saved_groups, w_in_g, w_out_g))
    return combine_rows(grad_in, outputs, routes, rows_at, weights)


def reference(entering, saved, routes, gates, w_in, w_out):
    current = entering
    collected = []
    for tick_idx in range(2):
        fwd_sel = slice(tick_idx % 2, None, 2)
        bwd_sel = slice(1 - tick_idx % 2, None, 2)
        fwd_part = lax.map(forward_map, (current[fwd_sel], routes[tick_idx][fwd_sel], gates[tick_idx][fwd_sel], w_in[fwd_sel], w_out[fwd_sel]))
        bwd_part = lax.map(backward_map, (current[bwd_sel], saved[bwd_sel], routes[tick_idx][bwd_sel], gates[tick_idx][bwd_sel], w_in[bwd_sel], w_out[bwd_sel]))
        layer_result = current.at[fwd_sel].set(fwd_part).at[bwd_sel].set(bwd_part)
        collected.append(layer_result)
        if tick_idx == 0:
            zero_block = jnp.zeros((1, TOKENS, D), jnp.bfloat16)
            from_above = jnp.concatenate([layer_result[1:], zero_block], axis=0)
            from_below = jnp.concatenate([zero_block, layer_result[:-1]], axis=0)
            even_section = (jnp.arange(SECTIONS, dtype=jnp.int32) % 2 == 0)[:, None, None]
            current = jnp.where(even_section, from_above, from_below)
    return jnp.stack(collected)
```

```python
import functools

import jax
import jax.numpy as jnp
from jax import lax
from jax.experimental import pallas as pl
from jax.experimental.pallas import tpu as pltpu
from jax.sharding import PartitionSpec as P

SHARDS = 8
CHIPS = 4
CHUNKS = 4
MESH = pl.DeviceIdType.MESH
F32 = jnp.float32
BF16 = jnp.bfloat16


def silu_slope(gate_vals):
    sigmoid_vals = jax.nn.sigmoid(gate_vals)
    return sigmoid_vals * (1.0 + gate_vals * (1.0 - sigmoid_vals))


def nn(a, b):
    return jnp.dot(a, b, preferred_element_type=F32)


def nt(a, b):
    return lax.dot_general(a, b, (((1,), (1,)), ((), ())), preferred_element_type=F32)


def tn(a, b):
    return lax.dot_general(a, b, (((0,), (0,)), ((), ())), preferred_element_type=F32)


def iota(shape, dim):
    return lax.broadcasted_iota(jnp.int32, shape, dim)


def wavefront(stages, chunks):
    for step in range(chunks + len(stages) - 1):
        for number in reversed(range(len(stages))):
            if 0 <= step - number < chunks:
                stages[number](step - number)


def kernel(
    experts, cap, cp, entering, routes, gates, saved_hbm, w_in_hbm, w_out_hbm, out,
    w_in, w_out, saved, silu_g, slope_u, acc, act, place, merge,
    gbuf, rbuf, agbuf, pbuf, sibbuf, qbuf, rsbuf, ubuf, vbuf, xbuf,
    load_sem, cross_s, cross_r, ag_s, ag_r, fw_s, fw_r, sib_s, sib_r,
    rs_s, rs_r, ret_s, ret_r, x_s, x_r,
):
    sec = lax.axis_index("section")
    me = lax.axis_index("expert")
    e, j = lax.div(me, SHARDS), lax.rem(me, SHARDS)
    q, c = lax.div(j, 2), lax.rem(j, 2)
    parity = lax.rem(sec, 2)
    tok, width = entering.shape
    dk = width // CHUNKS
    rows = experts * cap
    half = CHIPS * rows
    hdev = w_out.shape[0]

    def at_expert(o):
        return (sec, lax.rem(e + o, experts) * SHARDS + j)

    def at_chip(o):
        return (sec, e * SHARDS + lax.rem(q + o, CHIPS) * 2 + c)

    sibling = (sec, me + 1 - 2 * c)
    partner = (sec + 1 - 2 * parity, me)

    loads = [
        pltpu.make_async_copy(src, dst, load_sem.at[i])
        for i, (src, dst) in enumerate(
            ((saved_hbm, saved), (w_in_hbm, w_in), (w_out_hbm, w_out))
        )
    ]
    for load in loads:
        load.start()

    barrier = pltpu.get_barrier_semaphore()
    greeted = (
        [at_expert(o) for o in range(1, experts)]
        + [at_chip(o) for o in range(1, CHIPS)]
        + [sibling, partner]
    )
    for device in greeted:
        pl.semaphore_signal(barrier, inc=1, device_id=device, device_id_type=MESH)

    earlier = (iota((tok, tok), 1) < iota((tok, tok), 0)).astype(BF16)
    for tick in range(2):
        onehot = (routes[tick] == iota((tok, 128), 1)).astype(F32)
        before = nn(earlier, onehot.astype(BF16))
        slot = jnp.sum(before * onehot, axis=1, keepdims=True).astype(jnp.int32)
        target = routes[tick] * cp + slot
        place[tick] = (target == iota((tok, experts * cp), 1)).astype(F32).astype(BF16)
    r = iota((rows, experts * cp), 0)
    merge[...] = (
        (r // cap * cp + r % cap == iota((rows, experts * cp), 1)).astype(F32).astype(BF16)
    )

    pl.semaphore_wait(barrier, len(greeted))

    def copy(src, dst, send, recv, device):
        return pltpu.make_async_remote_copy(
            src_ref=src, dst_ref=dst, send_sem=send, recv_sem=recv,
            device_id=device, device_id_type=MESH,
        )

    sent = []

    def send(src, dst, send_sem, recv_sem, device):
        one = copy(src, dst, send_sem, recv_sem, device)
        one.start()
        sent.append(one)

    def arrive(dst, send_sem, recv_sem, device):
        copy(dst, dst, send_sem, recv_sem, device).wait_recv()

    def ds(index, size):
        return pl.ds(pl.multiple_of(index * size, size), size)

    def cols(k):
        return slice(k * dk, (k + 1) * dk)

    def tokens(t, k):
        return entering[:, cols(k)] if t == 0 else xbuf[k]

    def prepare_saved():
        for load in loads:
            load.wait()
        total = SHARDS * rows
        r = iota((total, total), 0)
        block, inner = r // rows, r % rows
        source_j = block % CHIPS * 2 + block // CHIPS
        column = (inner // cap * SHARDS + source_j) * cap + inner % cap
        perm = (column == iota((total, total), 1)).astype(F32).astype(BF16)
        ordered = nn(perm, saved[...])
        gate_vals, up_vals = ordered[:, :hdev], ordered[:, hdev:]
        silu_g[...] = jax.nn.silu(gate_vals)
        slope_u[...] = up_vals * silu_slope(gate_vals)

    def dispatch(t, forward):
        def spread(k):
            if t == 1:
                arrive(xbuf.at[k], x_s.at[k], x_r.at[k], partner)
            gbuf[t, k] = tn(place[t], tokens(t, k)).astype(BF16)
            for o in range(1, experts):
                send(
                    gbuf.at[t, k, ds(lax.rem(e + o, experts), cp)],
                    rbuf.at[t, k, ds(e, cp)],
                    cross_s.at[t, k, o], cross_r.at[t, k, o], at_expert(o),
                )
            rbuf[t, k, ds(e, cp)] = gbuf[t, k, ds(e, cp)]

        def gather(k):
            for o in range(1, experts):
                arrive(
                    rbuf.at[t, k, ds(lax.rem(e + experts - o, experts), cp)],
                    cross_s.at[t, k, o], cross_r.at[t, k, o], at_expert(o),
                )
            mine = ds(c * CHIPS + q, rows)
            agbuf[t, k, mine] = nn(merge[...], rbuf[t, k]).astype(BF16)
            for o in range(1, CHIPS):
                send(
                    agbuf.at[t, k, mine], agbuf.at[t, k, mine],
                    ag_s.at[t, k, o], ag_r.at[t, k, o], at_chip(o),
                )

        def forward_on(k):
            for o in range(1, CHIPS):
                arrive(
                    agbuf.at[t, k, ds(c * CHIPS + lax.rem(q + CHIPS - o, CHIPS), rows)],
                    ag_s.at[t, k, o], ag_r.at[t, k, o], at_chip(o),
                )
            send(
                agbuf.at[t, k, ds(c, half)], agbuf.at[t, k, ds(c, half)],
                fw_s.at[t, k], fw_r.at[t, k], sibling,
            )

        def multiply(k):
            if t == 0 and k == 0:
                prepare_saved()
            arrive(agbuf.at[t, k, ds(1 - c, half)], fw_s.at[t, k], fw_r.at[t, k], sibling)

            @pl.when(forward)
            def _():
                part = nn(agbuf[t, k], w_in[cols(k), :])
                acc[...] = part if k == 0 else acc[...] + part

            @pl.when(jnp.logical_not(forward))
            def _():
                part = nt(agbuf[t, k], w_out[:, cols(k)])
                acc[:, :hdev] = part if k == 0 else acc[:, :hdev] + part

            if k == CHUNKS - 1:
                activate(forward)

        return [spread, gather, forward_on, multiply]

    def activate(forward):
        @pl.when(forward)
        def _():
            hidden = jax.nn.silu(acc[:, :hdev]) * acc[:, hdev:]
            act[:, :hdev] = hidden.astype(BF16)

        @pl.when(jnp.logical_not(forward))
        def _():
            d_hidden = acc[:, :hdev]
            act[:, :hdev] = (d_hidden * slope_u[...]).astype(BF16)
            act[:, hdev:] = (d_hidden * silu_g[...]).astype(BF16)

    def give_back(t, forward):
        def part(k):
            @pl.when(forward)
            def _():
                pbuf[t, k] = nn(act[:, :hdev], w_out[:, cols(k)]).astype(BF16)

            @pl.when(jnp.logical_not(forward))
            def _():
                pbuf[t, k] = nt(act[...], w_in[cols(k), :]).astype(BF16)

            send(
                pbuf.at[t, k, ds(1 - c, half)], sibbuf.at[t, k],
                sib_s.at[t, k], sib_r.at[t, k], sibling,
            )

        def scatter(k):
            arrive(sibbuf.at[t, k], sib_s.at[t, k], sib_r.at[t, k], sibling)
            both = pbuf[t, k, ds(c, half)].astype(F32) + sibbuf[t, k].astype(F32)
            qbuf[t, k] = both.astype(BF16)
            for o in range(1, CHIPS):
                send(
                    qbuf.at[t, k, ds(lax.rem(q + o, CHIPS), rows)], rsbuf.at[t, k, o],
                    rs_s.at[t, k, o], rs_r.at[t, k, o], at_chip(o),
                )

        def return_on(k):
            total = qbuf[t, k, ds(q, rows)].astype(F32)
            for o in range(1, CHIPS):
                arrive(rsbuf.at[t, k, o], rs_s.at[t, k, o], rs_r.at[t, k, o], at_chip(o))
                total = total + rsbuf[t, k, o].astype(F32)
            ubuf[t, k] = tn(merge[...], total.astype(BF16)).astype(BF16)
            for o in range(1, experts):
                send(
                    ubuf.at[t, k, ds(lax.rem(e + o, experts), cp)],
                    vbuf.at[t, k, ds(e, cp)],
                    ret_s.at[t, k, o], ret_r.at[t, k, o], at_expert(o),
                )
            vbuf[t, k, ds(e, cp)] = ubuf[t, k, ds(e, cp)]

        def combine(k):
            for o in range(1, experts):
                arrive(
                    vbuf.at[t, k, ds(lax.rem(e + experts - o, experts), cp)],
                    ret_s.at[t, k, o], ret_r.at[t, k, o], at_expert(o),
                )
            picked = nn(place[t], vbuf[t, k])
            result = (tokens(t, k).astype(F32) + gates[t] * picked).astype(BF16)
            out[t, :, cols(k)] = result
            if t == 0:
                stage_x[k] = result
                send(stage_x.at[k], xbuf.at[k], x_s.at[k], x_r.at[k], partner)

        return [part, scatter, return_on, combine]

    stage_x, xbuf = xbuf.at[0], xbuf.at[1]
    first, second = parity == 0, parity == 1
    wavefront(dispatch(0, first), CHUNKS)
    wavefront(give_back(0, first) + dispatch(1, second), CHUNKS)
    wavefront(give_back(1, second), CHUNKS)
    for one in sent:
        one.wait_send()


def shards(entering, saved, routes, gates, w_in, w_out):
    experts = lax.axis_size("expert") // SHARDS
    tok, width = entering.shape[1:]
    top = routes.shape[3]
    assert top == 1
    cap = min(tok, max(2, (3 * tok * top + 2 * experts - 1) // (2 * experts)))
    cp = -(-cap // 16) * 16
    rows = experts * cap
    total = SHARDS * rows
    half = CHIPS * rows
    hdev = w_out.shape[2]
    dk = width // CHUNKS
    steps = (2, CHUNKS)
    dma = pltpu.SemaphoreType.DMA
    vmem = pl.BlockSpec(memory_space=pltpu.VMEM)
    hbm = pl.BlockSpec(memory_space=pl.ANY)
    out = pl.pallas_call(
        functools.partial(kernel, experts, cap, cp),
        out_shape=jax.ShapeDtypeStruct((2, tok, width), BF16),
        in_specs=[vmem] * 3 + [hbm] * 3,
        out_specs=vmem,
        scratch_shapes=[
            pltpu.VMEM(w_in.shape[2:], BF16),
            pltpu.VMEM(w_out.shape[2:], BF16),
            pltpu.VMEM((total, 2 * hdev), BF16),
            pltpu.VMEM((total, hdev), F32),
            pltpu.VMEM((total, hdev), F32),
            pltpu.VMEM((total, 2 * hdev), F32),
            pltpu.VMEM((total, 2 * hdev), BF16),
            pltpu.VMEM((2, tok, experts * cp), BF16),
            pltpu.VMEM((rows, experts * cp), BF16),
            pltpu.VMEM(steps + (experts * cp, dk), BF16),
            pltpu.VMEM(steps + (experts * cp, dk), BF16),
            pltpu.VMEM(steps + (total, dk), BF16),
            pltpu.VMEM(steps + (total, dk), BF16),
            pltpu.VMEM(steps + (half, dk), BF16),
            pltpu.VMEM(steps + (half, dk), BF16),
            pltpu.VMEM(steps + (CHIPS, rows, dk), BF16),
            pltpu.VMEM(steps + (experts * cp, dk), BF16),
            pltpu.VMEM(steps + (experts * cp, dk), BF16),
            pltpu.VMEM(steps + (tok, dk), BF16),
            dma((3,)),
            dma(steps + (experts,)), dma(steps + (experts,)),
            dma(steps + (CHIPS,)), dma(steps + (CHIPS,)),
            dma(steps), dma(steps),
            dma(steps), dma(steps),
            dma(steps + (CHIPS,)), dma(steps + (CHIPS,)),
            dma(steps + (experts,)), dma(steps + (experts,)),
            dma((CHUNKS,)), dma((CHUNKS,)),
        ],
        compiler_params=pltpu.CompilerParams(
            collective_id=0, has_side_effects=True, vmem_limit_bytes=56 * 1024 * 1024
        ),
    )(
        entering[0], routes[:, 0], gates[:, 0], saved[0, 0], w_in[0, 0], w_out[0, 0]
    )
    return out[:, None]


def solution(mesh):
    return jax.shard_map(
        shards,
        mesh=mesh,
        in_specs=(
            P("section", "expert", None),
            P("section", "expert", None, None),
            P(None, "section", "expert", None),
            P(None, "section", "expert", None),
            P("section", "expert", None, None),
            P("section", "expert", None, None),
        ),
        out_specs=P(None, "section", "expert", None),
        check_vma=False,
    )
```

```python
import functools

import jax
import jax.numpy as jnp
from jax import lax
from jax.experimental import pallas as pl
from jax.experimental.pallas import tpu as pltpu
from jax.sharding import PartitionSpec as P

SHARDS = 8
CHUNKS = 7
MESH = pl.DeviceIdType.MESH
F32 = jnp.float32
BF16 = jnp.bfloat16


def silu_slope(gate_vals):
    sigmoid_vals = jax.nn.sigmoid(gate_vals)
    return sigmoid_vals * (1.0 + gate_vals * (1.0 - sigmoid_vals))


def nn(a, b):
    return jnp.dot(a, b, preferred_element_type=F32)


def nt(a, b):
    return lax.dot_general(a, b, (((1,), (1,)), ((), ())), preferred_element_type=F32)


def tn(a, b):
    return lax.dot_general(a, b, (((0,), (0,)), ((), ())), preferred_element_type=F32)


def iota(shape, dim):
    return lax.broadcasted_iota(jnp.int32, shape, dim)


def wavefront(stages, chunks):
    starts = [0] + [number + 1 for number in range(1, len(stages))]
    for step in range(chunks + starts[-1]):
        for stage, start in reversed(list(zip(stages, starts))):
            if 0 <= step - start < chunks:
                stage(step - start)


def kernel(
    experts, cap, cp, entering, routes, gates, saved_hbm, w_in_hbm, w_out_hbm, out,
    w_in, w_out, saved, silu_g, slope_u, acc, act, place, merge,
    gbuf, rbuf, agbuf, pbuf, sibbuf, qbuf, ybuf, hbuf, zbuf, ubuf, vbuf, xbuf,
    load_sem, cross_s, cross_r, ret_s, ret_r, x_s, x_r, hop_s, hop_r,
):
    sec = lax.axis_index("section")
    me = lax.axis_index("expert")
    e, j = lax.div(me, SHARDS), lax.rem(me, SHARDS)
    z, y, c = lax.div(j, 4), lax.rem(lax.div(j, 2), 2), lax.rem(j, 2)
    parity = lax.rem(sec, 2)
    tok, width = entering.shape
    dk = width // CHUNKS
    rows = experts * cap
    quarter, half = 2 * rows, 4 * rows
    hdev = w_out.shape[0]

    def at_expert(o):
        return (sec, lax.rem(e + o, experts) * SHARDS + j)

    sibling = (sec, me + 1 - 2 * c)
    across_y = (sec, me + 2 - 4 * y)
    across_z = (sec, me + 4 - 8 * z)
    partner = (sec + 1 - 2 * parity, me)

    loads = [
        pltpu.make_async_copy(src, dst, load_sem.at[i])
        for i, (src, dst) in enumerate(
            ((saved_hbm, saved), (w_in_hbm, w_in), (w_out_hbm, w_out))
        )
    ]
    for load in loads:
        load.start()

    barrier = pltpu.get_barrier_semaphore()
    greeted = [at_expert(o) for o in range(1, experts)]
    greeted += [sibling, across_y, across_z, partner]
    for device in greeted:
        pl.semaphore_signal(barrier, inc=1, device_id=device, device_id_type=MESH)

    earlier = (iota((tok, tok), 1) < iota((tok, tok), 0)).astype(BF16)
    for tick in range(2):
        onehot = (routes[tick] == iota((tok, 128), 1)).astype(F32)
        before = nn(earlier, onehot.astype(BF16))
        slot = jnp.sum(before * onehot, axis=1, keepdims=True).astype(jnp.int32)
        target = routes[tick] * cp + slot
        place[tick] = (target == iota((tok, experts * cp), 1)).astype(F32).astype(BF16)
    r = iota((rows, experts * cp), 0)
    merge[...] = (
        (r // cap * cp + r % cap == iota((rows, experts * cp), 1)).astype(F32).astype(BF16)
    )

    pl.semaphore_wait(barrier, len(greeted))

    def copy(src, dst, send, recv, device):
        return pltpu.make_async_remote_copy(
            src_ref=src, dst_ref=dst, send_sem=send, recv_sem=recv,
            device_id=device, device_id_type=MESH,
        )

    sent = []

    def send(src, dst, send_sem, recv_sem, device):
        one = copy(src, dst, send_sem, recv_sem, device)
        one.start()
        sent.append(one)

    def arrive(dst, send_sem, recv_sem, device):
        copy(dst, dst, send_sem, recv_sem, device).wait_recv()

    def hop(src, dst, t, k, number, device):
        send(src, dst, hop_s.at[t, k, number], hop_r.at[t, k, number], device)

    def landed(dst, t, k, number, device):
        arrive(dst, hop_s.at[t, k, number], hop_r.at[t, k, number], device)

    def ds(index, size):
        return pl.ds(pl.multiple_of(index * size, size), size)

    def cols(k):
        return slice(k * dk, (k + 1) * dk)

    def tokens(t, k):
        return entering[:, cols(k)] if t == 0 else xbuf[k]

    def prepare_saved():
        loads[0].wait()
        total = SHARDS * rows
        r = iota((total, total), 0)
        block, inner = r // rows, r % rows
        source_j = block % 2 * 4 + block // 2 % 2 * 2 + block // 4
        column = (inner // cap * SHARDS + source_j) * cap + inner % cap
        perm = (column == iota((total, total), 1)).astype(F32).astype(BF16)
        ordered = nn(perm, saved[...])
        gate_vals, up_vals = ordered[:, :hdev], ordered[:, hdev:]
        silu_g[...] = jax.nn.silu(gate_vals)
        slope_u[...] = up_vals * silu_slope(gate_vals)

    def dispatch(t, forward):
        def spread(k):
            if t == 1:
                arrive(xbuf.at[k], x_s.at[k], x_r.at[k], partner)
            gbuf[t, k] = tn(place[t], tokens(t, k)).astype(BF16)
            for o in range(1, experts):
                send(
                    gbuf.at[t, k, ds(lax.rem(e + o, experts), cp)],
                    rbuf.at[t, k, ds(e, cp)],
                    cross_s.at[t, k, o], cross_r.at[t, k, o], at_expert(o),
                )
            rbuf[t, k, ds(e, cp)] = gbuf[t, k, ds(e, cp)]
            if t == 0 and k == 1:
                prepare_saved()

        def gather(k):
            for o in range(1, experts):
                arrive(
                    rbuf.at[t, k, ds(lax.rem(e + experts - o, experts), cp)],
                    cross_s.at[t, k, o], cross_r.at[t, k, o], at_expert(o),
                )
            own = ds(c * 4 + y * 2 + z, rows)
            agbuf[t, k, own] = nn(merge[...], rbuf[t, k]).astype(BF16)
            hop(agbuf.at[t, k, own], agbuf.at[t, k, own], t, k, 0, across_z)

        def over_y(k):
            landed(agbuf.at[t, k, ds(c * 4 + y * 2 + 1 - z, rows)], t, k, 0, across_z)
            pair = agbuf.at[t, k, ds(c * 2 + y, quarter)]
            hop(pair, pair, t, k, 1, across_y)

        def over_core(k):
            landed(agbuf.at[t, k, ds(c * 2 + 1 - y, quarter)], t, k, 1, across_y)
            mine = agbuf.at[t, k, ds(c, half)]
            hop(mine, mine, t, k, 2, sibling)

        def multiply(k):
            if t == 0 and k == 0:
                loads[1].wait()
                loads[2].wait()
            landed(agbuf.at[t, k, ds(1 - c, half)], t, k, 2, sibling)

            @pl.when(forward)
            def _():
                part = nn(agbuf[t, k], w_in[cols(k), :])
                acc[...] = part if k == 0 else acc[...] + part

            @pl.when(jnp.logical_not(forward))
            def _():
                part = nt(agbuf[t, k], w_out[:, cols(k)])
                acc[:, :hdev] = part if k == 0 else acc[:, :hdev] + part

            if k == CHUNKS - 1:
                activate(forward)

        return [spread, gather, over_y, over_core, multiply]

    def activate(forward):
        @pl.when(forward)
        def _():
            hidden = jax.nn.silu(acc[:, :hdev]) * acc[:, hdev:]
            act[:, :hdev] = hidden.astype(BF16)

        @pl.when(jnp.logical_not(forward))
        def _():
            d_hidden = acc[:, :hdev]
            act[:, :hdev] = (d_hidden * slope_u[...]).astype(BF16)
            act[:, hdev:] = (d_hidden * silu_g[...]).astype(BF16)

    def give_back(t, forward):
        def part(k):
            @pl.when(forward)
            def _():
                pbuf[t, k] = nn(act[:, :hdev], w_out[:, cols(k)]).astype(BF16)

            @pl.when(jnp.logical_not(forward))
            def _():
                pbuf[t, k] = nt(act[...], w_in[cols(k), :]).astype(BF16)

            hop(pbuf.at[t, k, ds(1 - c, half)], sibbuf.at[t, k], t, k, 3, sibling)

        def scatter_y(k):
            landed(sibbuf.at[t, k], t, k, 3, sibling)
            both = pbuf[t, k, ds(c, half)].astype(F32) + sibbuf[t, k].astype(F32)
            qbuf[t, k] = both.astype(BF16)
            hop(qbuf.at[t, k, ds(1 - y, quarter)], ybuf.at[t, k], t, k, 4, across_y)

        def scatter_z(k):
            landed(ybuf.at[t, k], t, k, 4, across_y)
            both = qbuf[t, k, ds(y, quarter)].astype(F32) + ybuf[t, k].astype(F32)
            hbuf[t, k] = both.astype(BF16)
            hop(hbuf.at[t, k, ds(1 - z, rows)], zbuf.at[t, k], t, k, 5, across_z)

        def return_on(k):
            landed(zbuf.at[t, k], t, k, 5, across_z)
            total = hbuf[t, k, ds(z, rows)].astype(F32) + zbuf[t, k].astype(F32)
            ubuf[t, k] = tn(merge[...], total.astype(BF16)).astype(BF16)
            for o in range(1, experts):
                send(
                    ubuf.at[t, k, ds(lax.rem(e + o, experts), cp)],
                    vbuf.at[t, k, ds(e, cp)],
                    ret_s.at[t, k, o], ret_r.at[t, k, o], at_expert(o),
                )
            vbuf[t, k, ds(e, cp)] = ubuf[t, k, ds(e, cp)]

        def combine(k):
            for o in range(1, experts):
                arrive(
                    vbuf.at[t, k, ds(lax.rem(e + experts - o, experts), cp)],
                    ret_s.at[t, k, o], ret_r.at[t, k, o], at_expert(o),
                )
            picked = nn(place[t], vbuf[t, k])
            result = (tokens(t, k).astype(F32) + gates[t] * picked).astype(BF16)
            out[t, :, cols(k)] = result
            if t == 0:
                stage_x[k] = result
                send(stage_x.at[k], xbuf.at[k], x_s.at[k], x_r.at[k], partner)

        return [part, scatter_y, scatter_z, return_on, combine]

    stage_x, xbuf = xbuf.at[0], xbuf.at[1]
    first, second = parity == 0, parity == 1
    wavefront(dispatch(0, first), CHUNKS)
    wavefront(give_back(0, first) + dispatch(1, second), CHUNKS)
    wavefront(give_back(1, second), CHUNKS)
    for one in sent:
        one.wait_send()


def shards(entering, saved, routes, gates, w_in, w_out):
    experts = lax.axis_size("expert") // SHARDS
    tok, width = entering.shape[1:]
    top = routes.shape[3]
    assert top == 1
    cap = min(tok, max(2, (3 * tok * top + 2 * experts - 1) // (2 * experts)))
    cp = -(-cap // 16) * 16
    rows = experts * cap
    total = SHARDS * rows
    quarter, half = 2 * rows, 4 * rows
    hdev = w_out.shape[2]
    dk = width // CHUNKS
    steps = (2, CHUNKS)
    dma = pltpu.SemaphoreType.DMA
    vmem = pl.BlockSpec(memory_space=pltpu.VMEM)
    hbm = pl.BlockSpec(memory_space=pl.ANY)
    out = pl.pallas_call(
        functools.partial(kernel, experts, cap, cp),
        out_shape=jax.ShapeDtypeStruct((2, tok, width), BF16),
        in_specs=[vmem] * 3 + [hbm] * 3,
        out_specs=vmem,
        scratch_shapes=[
            pltpu.VMEM(w_in.shape[2:], BF16),
            pltpu.VMEM(w_out.shape[2:], BF16),
            pltpu.VMEM((total, 2 * hdev), BF16),
            pltpu.VMEM((total, hdev), F32),
            pltpu.VMEM((total, hdev), F32),
            pltpu.VMEM((total, 2 * hdev), F32),
            pltpu.VMEM((total, 2 * hdev), BF16),
            pltpu.VMEM((2, tok, experts * cp), BF16),
            pltpu.VMEM((rows, experts * cp), BF16),
            pltpu.VMEM(steps + (experts * cp, dk), BF16),
            pltpu.VMEM(steps + (experts * cp, dk), BF16),
            pltpu.VMEM(steps + (total, dk), BF16),
            pltpu.VMEM(steps + (total, dk), BF16),
            pltpu.VMEM(steps + (half, dk), BF16),
            pltpu.VMEM(steps + (half, dk), BF16),
            pltpu.VMEM(steps + (quarter, dk), BF16),
            pltpu.VMEM(steps + (quarter, dk), BF16),
            pltpu.VMEM(steps + (rows, dk), BF16),
            pltpu.VMEM(steps + (experts * cp, dk), BF16),
            pltpu.VMEM(steps + (experts * cp, dk), BF16),
            pltpu.VMEM(steps + (tok, dk), BF16),
            dma((3,)),
            dma(steps + (experts,)), dma(steps + (experts,)),
            dma(steps + (experts,)), dma(steps + (experts,)),
            dma((CHUNKS,)), dma((CHUNKS,)),
            dma(steps + (6,)), dma(steps + (6,)),
        ],
        compiler_params=pltpu.CompilerParams(
            collective_id=0, has_side_effects=True, vmem_limit_bytes=56 * 1024 * 1024
        ),
    )(
        entering[0], routes[:, 0], gates[:, 0], saved[0, 0], w_in[0, 0], w_out[0, 0]
    )
    return out[:, None]


def solution(mesh):
    return jax.shard_map(
        shards,
        mesh=mesh,
        in_specs=(
            P("section", "expert", None),
            P("section", "expert", None, None),
            P(None, "section", "expert", None),
            P(None, "section", "expert", None),
            P("section", "expert", None, None),
            P("section", "expert", None, None),
        ),
        out_specs=P(None, "section", "expert", None),
        check_vma=False,
    )
```

```python
import functools

import jax
import jax.numpy as jnp
from jax import lax
from jax.experimental import pallas as pl
from jax.experimental.pallas import tpu as pltpu
from jax.sharding import PartitionSpec as P

SHARDS = 8
CHIPS = 4
CHUNKS = 7
HOP_US = 1.5
STEP_US = 0.3
LINK_RATE = {"y": 5e4, "z": 5e4, "mid": 5e4, "x": 5e4, "core": 6e5}
MESH = pl.DeviceIdType.MESH
F32 = jnp.float32
BF16 = jnp.bfloat16


def silu_slope(gate_vals):
    sigmoid_vals = jax.nn.sigmoid(gate_vals)
    return sigmoid_vals * (1.0 + gate_vals * (1.0 - sigmoid_vals))


def nn(a, b):
    return jnp.dot(a, b, preferred_element_type=F32)


def nt(a, b):
    return lax.dot_general(a, b, (((1,), (1,)), ((), ())), preferred_element_type=F32)


def tn(a, b):
    return lax.dot_general(a, b, (((0,), (0,)), ((), ())), preferred_element_type=F32)


def iota(shape, dim):
    return lax.broadcasted_iota(jnp.int32, shape, dim)


def listed(stages, chunks, row_bytes):
    now, free, done = 0.0, {}, [0] * len(stages)
    arrival = {(0, k): 0.0 for k in range(chunks)}
    for _ in range(len(stages) * chunks):
        open_now = [
            (number, k) for number, k in enumerate(done) if k < chunks and (number, k) in arrival
        ]
        ready = [item for item in open_now if arrival[item] <= now]
        number, k = max(ready) if ready else min(open_now, key=lambda item: arrival[item])
        stage, work, sends = stages[number]
        stage(k)
        done[number] += 1
        now = max(now, arrival[number, k]) + STEP_US + work / chunks
        arrived = now
        for link, rows in sends:
            free[link] = max(now, free.get(link, 0.0)) + rows * row_bytes / LINK_RATE[link]
            arrived = max(arrived, free[link] + HOP_US)
        arrival[number + 1, k] = arrived


def kernel(
    experts, cap, cp, entering, routes, gates, saved_hbm, w_in_hbm, w_out_hbm, out,
    w_in, w_out, saved, silu_g, slope_u, acc, act, weight, place, merge,
    gbuf, rbuf, agbuf, pbuf, sibbuf, qbuf, rsbuf, ubuf, vbuf, xbuf,
    load_sem, cross_s, cross_r, ag_s, ag_r, fw_s, fw_r, sib_s, sib_r,
    rs_s, rs_r, ret_s, ret_r, x_s, x_r,
):
    sec = lax.axis_index("section")
    me = lax.axis_index("expert")
    e, j = lax.div(me, SHARDS), lax.rem(me, SHARDS)
    q, c = lax.div(j, 2), lax.rem(j, 2)
    parity = lax.rem(sec, 2)
    tok, width = entering.shape
    dk = width // CHUNKS
    rows = experts * cap
    half = CHIPS * rows
    hdev = w_out.shape[0]

    def at_expert(o):
        return (sec, lax.rem(e + o, experts) * SHARDS + j)

    def at_chip(o):
        return (sec, e * SHARDS + lax.rem(q + o, CHIPS) * 2 + c)

    sibling = (sec, me + 1 - 2 * c)
    partner = (sec + 1 - 2 * parity, me)

    loads = [
        pltpu.make_async_copy(src, dst, load_sem.at[i])
        for i, (src, dst) in enumerate(
            ((saved_hbm, saved), (w_in_hbm, w_in), (w_out_hbm, w_out))
        )
    ]
    for load in loads:
        load.start()

    barrier = pltpu.get_barrier_semaphore()
    greeted = (
        [at_expert(o) for o in range(1, experts)]
        + [at_chip(o) for o in range(1, CHIPS)]
        + [sibling, partner]
    )
    for device in greeted:
        pl.semaphore_signal(barrier, inc=1, device_id=device, device_id_type=MESH)

    earlier = (iota((tok, tok), 1) < iota((tok, tok), 0)).astype(BF16)
    same = iota((tok, tok), 1) == iota((tok, tok), 0)

    def column(row):
        return jnp.sum(jnp.where(same, row.astype(F32), 0.0), axis=1, keepdims=True)

    for tick in range(2):
        route = column(routes[tick]).astype(jnp.int32)
        weight[tick] = column(gates[tick])
        onehot = (route == iota((tok, 128), 1)).astype(F32)
        before = nn(earlier, onehot.astype(BF16))
        slot = jnp.sum(before * onehot, axis=1, keepdims=True).astype(jnp.int32)
        target = route * cp + slot
        place[tick] = (target == iota((tok, experts * cp), 1)).astype(F32).astype(BF16)
    r = iota((rows, experts * cp), 0)
    merge[...] = (
        (r // cap * cp + r % cap == iota((rows, experts * cp), 1)).astype(F32).astype(BF16)
    )

    pl.semaphore_wait(barrier, len(greeted))

    def copy(src, dst, send, recv, device):
        return pltpu.make_async_remote_copy(
            src_ref=src, dst_ref=dst, send_sem=send, recv_sem=recv,
            device_id=device, device_id_type=MESH,
        )

    sent = []

    def send(src, dst, send_sem, recv_sem, device):
        one = copy(src, dst, send_sem, recv_sem, device)
        one.start()
        sent.append(one)

    def arrive(dst, send_sem, recv_sem, device):
        copy(dst, dst, send_sem, recv_sem, device).wait_recv()

    def ds(index, size):
        return pl.ds(pl.multiple_of(index * size, size), size)

    def cols(k):
        return slice(k * dk, (k + 1) * dk)

    def tokens(t, k):
        return entering[:, cols(k)] if t == 0 else xbuf[k]

    def prepare_saved():
        loads[0].wait()
        total = SHARDS * rows
        r = iota((total, total), 0)
        block, inner = r // rows, r % rows
        source_j = block % CHIPS * 2 + block // CHIPS
        column = (inner // cap * SHARDS + source_j) * cap + inner % cap
        perm = (column == iota((total, total), 1)).astype(F32).astype(BF16)
        ordered = nn(perm, saved[...])
        gate_vals, up_vals = ordered[:, :hdev], ordered[:, hdev:]
        silu_g[...] = jax.nn.silu(gate_vals)
        slope_u[...] = up_vals * silu_slope(gate_vals)

    def dispatch(t, forward):
        def spread(k):
            if t == 1:
                arrive(xbuf.at[k], x_s.at[k], x_r.at[k], partner)
            gbuf[t, k] = tn(place[t], tokens(t, k)).astype(BF16)
            for o in range(1, experts):
                send(
                    gbuf.at[t, k, ds(lax.rem(e + o, experts), cp)],
                    rbuf.at[t, k, ds(e, cp)],
                    cross_s.at[t, k, o], cross_r.at[t, k, o], at_expert(o),
                )
            rbuf[t, k, ds(e, cp)] = gbuf[t, k, ds(e, cp)]
            if t == 0 and k == 2:
                prepare_saved()

        def gather(k):
            for o in range(1, experts):
                arrive(
                    rbuf.at[t, k, ds(lax.rem(e + experts - o, experts), cp)],
                    cross_s.at[t, k, o], cross_r.at[t, k, o], at_expert(o),
                )
            mine = ds(c * CHIPS + q, rows)
            agbuf[t, k, mine] = nn(merge[...], rbuf[t, k]).astype(BF16)
            for o in range(1, CHIPS):
                send(
                    agbuf.at[t, k, mine], agbuf.at[t, k, mine],
                    ag_s.at[t, k, o], ag_r.at[t, k, o], at_chip(o),
                )

        def forward_on(k):
            for o in range(1, CHIPS):
                arrive(
                    agbuf.at[t, k, ds(c * CHIPS + lax.rem(q + CHIPS - o, CHIPS), rows)],
                    ag_s.at[t, k, o], ag_r.at[t, k, o], at_chip(o),
                )
            send(
                agbuf.at[t, k, ds(c, half)], agbuf.at[t, k, ds(c, half)],
                fw_s.at[t, k], fw_r.at[t, k], sibling,
            )

        def multiply(k):
            if t == 0 and k == 0:
                loads[1].wait()
                loads[2].wait()
            arrive(agbuf.at[t, k, ds(1 - c, half)], fw_s.at[t, k], fw_r.at[t, k], sibling)

            @pl.when(forward)
            def _():
                part = nn(agbuf[t, k], w_in[cols(k), :])
                acc[...] = part if k == 0 else acc[...] + part

            @pl.when(jnp.logical_not(forward))
            def _():
                part = nt(agbuf[t, k], w_out[:, cols(k)])
                acc[:, :hdev] = part if k == 0 else acc[:, :hdev] + part

            if k == CHUNKS - 1:
                activate(forward)

        return [
            (spread, 1.0, [("z", cp), ("mid", 2 * cp)]),
            (gather, 1.0, [("y", 2 * rows), ("z", 2 * rows)]),
            (forward_on, 0.0, [("core", half)]),
            (multiply, 4.0, []),
        ]

    def activate(forward):
        @pl.when(forward)
        def _():
            hidden = jax.nn.silu(acc[:, :hdev]) * acc[:, hdev:]
            act[:, :hdev] = hidden.astype(BF16)

        @pl.when(jnp.logical_not(forward))
        def _():
            d_hidden = acc[:, :hdev]
            act[:, :hdev] = (d_hidden * slope_u[...]).astype(BF16)
            act[:, hdev:] = (d_hidden * silu_g[...]).astype(BF16)

    def give_back(t, forward):
        def part(k):
            @pl.when(forward)
            def _():
                pbuf[t, k] = nn(act[:, :hdev], w_out[:, cols(k)]).astype(BF16)

            @pl.when(jnp.logical_not(forward))
            def _():
                pbuf[t, k] = nt(act[...], w_in[cols(k), :]).astype(BF16)

            send(
                pbuf.at[t, k, ds(1 - c, half)], sibbuf.at[t, k],
                sib_s.at[t, k], sib_r.at[t, k], sibling,
            )

        def scatter(k):
            arrive(sibbuf.at[t, k], sib_s.at[t, k], sib_r.at[t, k], sibling)
            both = pbuf[t, k, ds(c, half)].astype(F32) + sibbuf[t, k].astype(F32)
            qbuf[t, k] = both.astype(BF16)
            for o in range(1, CHIPS):
                send(
                    qbuf.at[t, k, ds(lax.rem(q + o, CHIPS), rows)], rsbuf.at[t, k, o],
                    rs_s.at[t, k, o], rs_r.at[t, k, o], at_chip(o),
                )

        def return_on(k):
            total = qbuf[t, k, ds(q, rows)].astype(F32)
            for o in range(1, CHIPS):
                arrive(rsbuf.at[t, k, o], rs_s.at[t, k, o], rs_r.at[t, k, o], at_chip(o))
                total = total + rsbuf[t, k, o].astype(F32)
            ubuf[t, k] = tn(merge[...], total.astype(BF16)).astype(BF16)
            for o in range(1, experts):
                send(
                    ubuf.at[t, k, ds(lax.rem(e + o, experts), cp)],
                    vbuf.at[t, k, ds(e, cp)],
                    ret_s.at[t, k, o], ret_r.at[t, k, o], at_expert(o),
                )
            vbuf[t, k, ds(e, cp)] = ubuf[t, k, ds(e, cp)]

        def combine(k):
            for o in range(1, experts):
                arrive(
                    vbuf.at[t, k, ds(lax.rem(e + experts - o, experts), cp)],
                    ret_s.at[t, k, o], ret_r.at[t, k, o], at_expert(o),
                )
            picked = nn(place[t], vbuf[t, k])
            result = (tokens(t, k).astype(F32) + weight[t] * picked).astype(BF16)
            out[t, :, cols(k)] = result
            if t == 0:
                stage_x[k] = result
                send(stage_x.at[k], xbuf.at[k], x_s.at[k], x_r.at[k], partner)

        return [
            (part, 4.0, [("core", half)]),
            (scatter, 1.5, [("y", 2 * rows), ("z", 2 * rows)]),
            (return_on, 1.0, [("z", cp), ("mid", 2 * cp)]),
            (combine, 0.7, [("x", tok)]),
        ]

    stage_x, xbuf = xbuf.at[0], xbuf.at[1]
    first, second = parity == 0, parity == 1
    listed(dispatch(0, first), CHUNKS, 2 * dk)
    listed(give_back(0, first) + dispatch(1, second), CHUNKS, 2 * dk)
    listed(give_back(1, second), CHUNKS, 2 * dk)
    for one in sent:
        one.wait_send()


def shards(entering, saved, routes, gates, w_in, w_out):
    experts = lax.axis_size("expert") // SHARDS
    tok, width = entering.shape[1:]
    top = routes.shape[3]
    assert top == 1
    cap = min(tok, max(2, (3 * tok * top + 2 * experts - 1) // (2 * experts)))
    cp = -(-cap // 16) * 16
    rows = experts * cap
    total = SHARDS * rows
    half = CHIPS * rows
    hdev = w_out.shape[2]
    dk = width // CHUNKS
    steps = (2, CHUNKS)
    dma = pltpu.SemaphoreType.DMA
    vmem = pl.BlockSpec(memory_space=pltpu.VMEM)
    hbm = pl.BlockSpec(memory_space=pl.ANY)
    out = pl.pallas_call(
        functools.partial(kernel, experts, cap, cp),
        out_shape=jax.ShapeDtypeStruct((2, tok, width), BF16),
        in_specs=[vmem] * 3 + [hbm] * 3,
        out_specs=vmem,
        scratch_shapes=[
            pltpu.VMEM(w_in.shape[2:], BF16),
            pltpu.VMEM(w_out.shape[2:], BF16),
            pltpu.VMEM((total, 2 * hdev), BF16),
            pltpu.VMEM((total, hdev), F32),
            pltpu.VMEM((total, hdev), F32),
            pltpu.VMEM((total, 2 * hdev), F32),
            pltpu.VMEM((total, 2 * hdev), BF16),
            pltpu.VMEM((2, tok, 1), F32),
            pltpu.VMEM((2, tok, experts * cp), BF16),
            pltpu.VMEM((rows, experts * cp), BF16),
            pltpu.VMEM(steps + (experts * cp, dk), BF16),
            pltpu.VMEM(steps + (experts * cp, dk), BF16),
            pltpu.VMEM(steps + (total, dk), BF16),
            pltpu.VMEM(steps + (total, dk), BF16),
            pltpu.VMEM(steps + (half, dk), BF16),
            pltpu.VMEM(steps + (half, dk), BF16),
            pltpu.VMEM(steps + (CHIPS, rows, dk), BF16),
            pltpu.VMEM(steps + (experts * cp, dk), BF16),
            pltpu.VMEM(steps + (experts * cp, dk), BF16),
            pltpu.VMEM(steps + (tok, dk), BF16),
            dma((3,)),
            dma(steps + (experts,)), dma(steps + (experts,)),
            dma(steps + (CHIPS,)), dma(steps + (CHIPS,)),
            dma(steps), dma(steps),
            dma(steps), dma(steps),
            dma(steps + (CHIPS,)), dma(steps + (CHIPS,)),
            dma(steps + (experts,)), dma(steps + (experts,)),
            dma((CHUNKS,)), dma((CHUNKS,)),
        ],
        compiler_params=pltpu.CompilerParams(
            collective_id=0, has_side_effects=True, vmem_limit_bytes=56 * 1024 * 1024
        ),
    )(
        entering[0], routes.reshape(2, 1, tok), gates.reshape(2, 1, tok),
        saved[0, 0], w_in[0, 0], w_out[0, 0],
    )
    return out[:, None]


def solution(mesh):
    return jax.shard_map(
        shards,
        mesh=mesh,
        in_specs=(
            P("section", "expert", None),
            P("section", "expert", None, None),
            P(None, "section", "expert", None),
            P(None, "section", "expert", None),
            P("section", "expert", None, None),
            P("section", "expert", None, None),
        ),
        out_specs=P(None, "section", "expert", None),
        check_vma=False,
    )
```

```python
import functools

import jax
import jax.numpy as jnp
from jax import lax
from jax.experimental import pallas as pl
from jax.experimental.pallas import tpu as pltpu
from jax.sharding import PartitionSpec as P

SHARDS = 8
CHIPS = 4
CHUNKS = 7
HOP_US = 1.5
STEP_US = 0.3
LINK_RATE = {"y": 5e4, "z": 5e4, "mid": 5e4, "x": 5e4, "core": 6e5}
MESH = pl.DeviceIdType.MESH
F32 = jnp.float32
BF16 = jnp.bfloat16


def silu_slope(gate_vals):
    sigmoid_vals = jax.nn.sigmoid(gate_vals)
    return sigmoid_vals * (1.0 + gate_vals * (1.0 - sigmoid_vals))


def nn(a, b):
    return jnp.dot(a, b, preferred_element_type=F32)


def nt(a, b):
    return lax.dot_general(a, b, (((1,), (1,)), ((), ())), preferred_element_type=F32)


def tn(a, b):
    return lax.dot_general(a, b, (((0,), (0,)), ((), ())), preferred_element_type=F32)


def iota(shape, dim):
    return lax.broadcasted_iota(jnp.int32, shape, dim)


def listed(stages, chunks, row_bytes):
    now, free, done = 0.0, {}, [0] * len(stages)
    arrival = {(0, k): 0.0 for k in range(chunks)}
    for _ in range(len(stages) * chunks):
        open_now = [
            (number, k) for number, k in enumerate(done) if k < chunks and (number, k) in arrival
        ]
        ready = [item for item in open_now if arrival[item] <= now]
        number, k = max(ready) if ready else min(open_now, key=lambda item: arrival[item])
        stage, work, sends = stages[number]
        stage(k)
        done[number] += 1
        now = max(now, arrival[number, k]) + STEP_US + work / chunks
        arrived = now
        for link, rows in sends:
            free[link] = max(now, free.get(link, 0.0)) + rows * row_bytes / LINK_RATE[link]
            arrived = max(arrived, free[link] + HOP_US)
        arrival[number + 1, k] = arrived


def kernel(
    experts, cap, fold, cp, entering, routes, gates, saved_hbm, w_in_hbm, w_out_hbm, out,
    w_in, w_out, saved, silu_g, slope_u, acc, act, weight, place, merge,
    gbuf, rbuf, agbuf, pbuf, sibbuf, qbuf, rsbuf, ubuf, vbuf, xbuf,
    load_sem, cross_s, cross_r, ag_s, ag_r, fw_s, fw_r, sib_s, sib_r,
    rs_s, rs_r, ret_s, ret_r, x_s, x_r,
):
    sec = lax.axis_index("section")
    me = lax.axis_index("expert")
    e, j = lax.div(me, SHARDS), lax.rem(me, SHARDS)
    q, c = lax.div(j, 2), lax.rem(j, 2)
    parity = lax.rem(sec, 2)
    tok, width = entering.shape
    dk = width // CHUNKS
    rows = experts * cap
    half = CHIPS * rows
    hdev = w_out.shape[0]

    def at_expert(o):
        return (sec, lax.rem(e + o, experts) * SHARDS + j)

    def at_chip(o):
        return (sec, e * SHARDS + lax.rem(q + o, CHIPS) * 2 + c)

    sibling = (sec, me + 1 - 2 * c)
    partner = (sec + 1 - 2 * parity, me)

    loads = [
        pltpu.make_async_copy(src, dst, load_sem.at[i])
        for i, (src, dst) in enumerate(
            ((saved_hbm, saved), (w_in_hbm, w_in), (w_out_hbm, w_out))
        )
    ]
    for load in loads:
        load.start()

    barrier = pltpu.get_barrier_semaphore()
    greeted = (
        [at_expert(o) for o in range(1, experts)]
        + [at_chip(o) for o in range(1, CHIPS)]
        + [sibling, partner]
    )
    for device in greeted:
        pl.semaphore_signal(barrier, inc=1, device_id=device, device_id_type=MESH)

    earlier = (iota((tok, tok), 1) < iota((tok, tok), 0)).astype(BF16)
    same = iota((tok, tok), 1) == iota((tok, tok), 0)

    def column(row):
        return jnp.sum(jnp.where(same, row.astype(F32), 0.0), axis=1, keepdims=True)

    for tick in range(2):
        route = column(routes[tick]).astype(jnp.int32)
        weight[tick] = column(gates[tick])
        onehot = (route == iota((tok, 128), 1)).astype(F32)
        before = nn(earlier, onehot.astype(BF16))
        slot = jnp.sum(before * onehot, axis=1, keepdims=True).astype(jnp.int32)
        for h in range(fold):
            target = route * cp + h * cap + slot
            spots = target == iota((tok, experts * cp), 1)
            place[tick, h] = spots.astype(F32).astype(BF16)
    r = iota((rows, experts * cp), 0)
    for h in range(fold):
        spots = r // cap * cp + h * cap + r % cap == iota((rows, experts * cp), 1)
        merge[h] = spots.astype(F32).astype(BF16)

    pl.semaphore_wait(barrier, len(greeted))

    def copy(src, dst, send, recv, device):
        return pltpu.make_async_remote_copy(
            src_ref=src, dst_ref=dst, send_sem=send, recv_sem=recv,
            device_id=device, device_id_type=MESH,
        )

    sent = []

    def send(src, dst, send_sem, recv_sem, device):
        one = copy(src, dst, send_sem, recv_sem, device)
        one.start()
        sent.append(one)

    def arrive(dst, send_sem, recv_sem, device):
        copy(dst, dst, send_sem, recv_sem, device).wait_recv()

    def ds(index, size):
        return pl.ds(pl.multiple_of(index * size, size), size)

    def cols(k):
        return slice(k * dk, (k + 1) * dk)

    def tokens(t, k):
        return entering[:, cols(k)] if t == 0 else xbuf[k]

    def part_of(h):
        return slice(h * dk // fold, (h + 1) * dk // fold)

    def folded(tables, data):
        total = tn(tables[0], data[:, part_of(0)])
        for h in range(1, fold):
            total = total + tn(tables[h], data[:, part_of(h)])
        return total.astype(BF16)

    def prepare_saved():
        loads[0].wait()
        total = SHARDS * rows
        r = iota((total, total), 0)
        block, inner = r // rows, r % rows
        source_j = block % CHIPS * 2 + block // CHIPS
        column = (inner // cap * SHARDS + source_j) * cap + inner % cap
        perm = (column == iota((total, total), 1)).astype(F32).astype(BF16)
        ordered = nn(perm, saved[...])
        gate_vals, up_vals = ordered[:, :hdev], ordered[:, hdev:]
        silu_g[...] = jax.nn.silu(gate_vals)
        slope_u[...] = up_vals * silu_slope(gate_vals)

    def dispatch(t, forward):
        def spread(k):
            if t == 1:
                arrive(xbuf.at[k], x_s.at[k], x_r.at[k], partner)
            gbuf[t, k] = folded(place[t], tokens(t, k))
            for o in range(1, experts):
                send(
                    gbuf.at[t, k, ds(lax.rem(e + o, experts), cp)],
                    rbuf.at[t, k, ds(e, cp)],
                    cross_s.at[t, k, o], cross_r.at[t, k, o], at_expert(o),
                )
            rbuf[t, k, ds(e, cp)] = gbuf[t, k, ds(e, cp)]
            if t == 0 and k == 2:
                prepare_saved()

        def gather(k):
            for o in range(1, experts):
                arrive(
                    rbuf.at[t, k, ds(lax.rem(e + experts - o, experts), cp)],
                    cross_s.at[t, k, o], cross_r.at[t, k, o], at_expert(o),
                )
            mine = ds(c * CHIPS + q, rows)
            for h in range(fold):
                agbuf[t, k, mine, part_of(h)] = nn(merge[h], rbuf[t, k]).astype(BF16)
            for o in range(1, CHIPS):
                send(
                    agbuf.at[t, k, mine], agbuf.at[t, k, mine],
                    ag_s.at[t, k, o], ag_r.at[t, k, o], at_chip(o),
                )

        def forward_on(k):
            for o in range(1, CHIPS):
                arrive(
                    agbuf.at[t, k, ds(c * CHIPS + lax.rem(q + CHIPS - o, CHIPS), rows)],
                    ag_s.at[t, k, o], ag_r.at[t, k, o], at_chip(o),
                )
            send(
                agbuf.at[t, k, ds(c, half)], agbuf.at[t, k, ds(c, half)],
                fw_s.at[t, k], fw_r.at[t, k], sibling,
            )

        def multiply(k):
            if t == 0 and k == 0:
                loads[1].wait()
                loads[2].wait()
            arrive(agbuf.at[t, k, ds(1 - c, half)], fw_s.at[t, k], fw_r.at[t, k], sibling)

            @pl.when(forward)
            def _():
                part = nn(agbuf[t, k], w_in[cols(k), :])
                acc[...] = part if k == 0 else acc[...] + part

            @pl.when(jnp.logical_not(forward))
            def _():
                part = nt(agbuf[t, k], w_out[:, cols(k)])
                acc[:, :hdev] = part if k == 0 else acc[:, :hdev] + part

            if k == CHUNKS - 1:
                activate(forward)

        return [
            (spread, 1.0, [("z", cp // fold), ("mid", 2 * cp // fold)]),
            (gather, 1.0, [("y", 2 * rows), ("z", 2 * rows)]),
            (forward_on, 0.0, [("core", half)]),
            (multiply, 4.0, []),
        ]

    def activate(forward):
        @pl.when(forward)
        def _():
            hidden = jax.nn.silu(acc[:, :hdev]) * acc[:, hdev:]
            act[:, :hdev] = hidden.astype(BF16)

        @pl.when(jnp.logical_not(forward))
        def _():
            d_hidden = acc[:, :hdev]
            act[:, :hdev] = (d_hidden * slope_u[...]).astype(BF16)
            act[:, hdev:] = (d_hidden * silu_g[...]).astype(BF16)

    def give_back(t, forward):
        def part(k):
            @pl.when(forward)
            def _():
                pbuf[t, k] = nn(act[:, :hdev], w_out[:, cols(k)]).astype(BF16)

            @pl.when(jnp.logical_not(forward))
            def _():
                pbuf[t, k] = nt(act[...], w_in[cols(k), :]).astype(BF16)

            send(
                pbuf.at[t, k, ds(1 - c, half)], sibbuf.at[t, k],
                sib_s.at[t, k], sib_r.at[t, k], sibling,
            )

        def scatter(k):
            arrive(sibbuf.at[t, k], sib_s.at[t, k], sib_r.at[t, k], sibling)
            both = pbuf[t, k, ds(c, half)].astype(F32) + sibbuf[t, k].astype(F32)
            qbuf[t, k] = both.astype(BF16)
            for o in range(1, CHIPS):
                send(
                    qbuf.at[t, k, ds(lax.rem(q + o, CHIPS), rows)], rsbuf.at[t, k, o],
                    rs_s.at[t, k, o], rs_r.at[t, k, o], at_chip(o),
                )

        def return_on(k):
            total = qbuf[t, k, ds(q, rows)].astype(F32)
            for o in range(1, CHIPS):
                arrive(rsbuf.at[t, k, o], rs_s.at[t, k, o], rs_r.at[t, k, o], at_chip(o))
                total = total + rsbuf[t, k, o].astype(F32)
            ubuf[t, k] = folded(merge[...], total.astype(BF16))
            for o in range(1, experts):
                send(
                    ubuf.at[t, k, ds(lax.rem(e + o, experts), cp)],
                    vbuf.at[t, k, ds(e, cp)],
                    ret_s.at[t, k, o], ret_r.at[t, k, o], at_expert(o),
                )
            vbuf[t, k, ds(e, cp)] = ubuf[t, k, ds(e, cp)]

        def combine(k):
            for o in range(1, experts):
                arrive(
                    vbuf.at[t, k, ds(lax.rem(e + experts - o, experts), cp)],
                    ret_s.at[t, k, o], ret_r.at[t, k, o], at_expert(o),
                )
            picked = jnp.concatenate([nn(place[t, h], vbuf[t, k]) for h in range(fold)], axis=1)
            result = (tokens(t, k).astype(F32) + weight[t] * picked).astype(BF16)
            out[t, :, cols(k)] = result
            if t == 0:
                stage_x[k] = result
                send(stage_x.at[k], xbuf.at[k], x_s.at[k], x_r.at[k], partner)

        return [
            (part, 4.0, [("core", half)]),
            (scatter, 1.5, [("y", 2 * rows), ("z", 2 * rows)]),
            (return_on, 1.0, [("z", cp // fold), ("mid", 2 * cp // fold)]),
            (combine, 0.7, [("x", tok)]),
        ]

    stage_x, xbuf = xbuf.at[0], xbuf.at[1]
    first, second = parity == 0, parity == 1
    listed(dispatch(0, first), CHUNKS, 2 * dk)
    listed(give_back(0, first) + dispatch(1, second), CHUNKS, 2 * dk)
    listed(give_back(1, second), CHUNKS, 2 * dk)
    for one in sent:
        one.wait_send()


def shards(entering, saved, routes, gates, w_in, w_out):
    experts = lax.axis_size("expert") // SHARDS
    tok, width = entering.shape[1:]
    top = routes.shape[3]
    assert top == 1
    cap = min(tok, max(2, (3 * tok * top + 2 * experts - 1) // (2 * experts)))
    fold = 2 if cap % 16 and 2 * cap % 16 == 0 else 1
    cp = -(-fold * cap // 16) * 16
    rows = experts * cap
    total = SHARDS * rows
    half = CHIPS * rows
    hdev = w_out.shape[2]
    dk = width // CHUNKS
    steps = (2, CHUNKS)
    dma = pltpu.SemaphoreType.DMA
    vmem = pl.BlockSpec(memory_space=pltpu.VMEM)
    hbm = pl.BlockSpec(memory_space=pl.ANY)
    out = pl.pallas_call(
        functools.partial(kernel, experts, cap, fold, cp),
        out_shape=jax.ShapeDtypeStruct((2, tok, width), BF16),
        in_specs=[vmem] * 3 + [hbm] * 3,
        out_specs=vmem,
        scratch_shapes=[
            pltpu.VMEM(w_in.shape[2:], BF16),
            pltpu.VMEM(w_out.shape[2:], BF16),
            pltpu.VMEM((total, 2 * hdev), BF16),
            pltpu.VMEM((total, hdev), F32),
            pltpu.VMEM((total, hdev), F32),
            pltpu.VMEM((total, 2 * hdev), F32),
            pltpu.VMEM((total, 2 * hdev), BF16),
            pltpu.VMEM((2, tok, 1), F32),
            pltpu.VMEM((2, fold, tok, experts * cp), BF16),
            pltpu.VMEM((fold, rows, experts * cp), BF16),
            pltpu.VMEM(steps + (experts * cp, dk // fold), BF16),
            pltpu.VMEM(steps + (experts * cp, dk // fold), BF16),
            pltpu.VMEM(steps + (total, dk), BF16),
            pltpu.VMEM(steps + (total, dk), BF16),
            pltpu.VMEM(steps + (half, dk), BF16),
            pltpu.VMEM(steps + (half, dk), BF16),
            pltpu.VMEM(steps + (CHIPS, rows, dk), BF16),
            pltpu.VMEM(steps + (experts * cp, dk // fold), BF16),
            pltpu.VMEM(steps + (experts * cp, dk // fold), BF16),
            pltpu.VMEM(steps + (tok, dk), BF16),
            dma((3,)),
            dma(steps + (experts,)), dma(steps + (experts,)),
            dma(steps + (CHIPS,)), dma(steps + (CHIPS,)),
            dma(steps), dma(steps),
            dma(steps), dma(steps),
            dma(steps + (CHIPS,)), dma(steps + (CHIPS,)),
            dma(steps + (experts,)), dma(steps + (experts,)),
            dma((CHUNKS,)), dma((CHUNKS,)),
        ],
        compiler_params=pltpu.CompilerParams(
            collective_id=0, has_side_effects=True, vmem_limit_bytes=56 * 1024 * 1024
        ),
    )(
        entering[0], routes.reshape(2, 1, tok), gates.reshape(2, 1, tok),
        saved[0, 0], w_in[0, 0], w_out[0, 0],
    )
    return out[:, None]


def solution(mesh):
    return jax.shard_map(
        shards,
        mesh=mesh,
        in_specs=(
            P("section", "expert", None),
            P("section", "expert", None, None),
            P(None, "section", "expert", None),
            P(None, "section", "expert", None),
            P("section", "expert", None, None),
            P("section", "expert", None, None),
        ),
        out_specs=P(None, "section", "expert", None),
        check_vma=False,
    )
```

```python
import functools

import jax
import jax.numpy as jnp
from jax import lax
from jax.experimental import pallas as pl
from jax.experimental.pallas import tpu as pltpu
from jax.sharding import PartitionSpec as P

SHARDS = 8
CHIPS = 4
CHUNKS = 7
HOP_US = 1.5
STEP_US = 0.3
LINK_RATE = {"y": 5e4, "z": 5e4, "mid": 5e4, "x": 5e4, "core": 6e5}
MESH = pl.DeviceIdType.MESH
F32 = jnp.float32
BF16 = jnp.bfloat16


def silu_slope(gate_vals):
    sigmoid_vals = jax.nn.sigmoid(gate_vals)
    return sigmoid_vals * (1.0 + gate_vals * (1.0 - sigmoid_vals))


def nn(a, b):
    return jnp.dot(a, b, preferred_element_type=F32)


def nt(a, b):
    return lax.dot_general(a, b, (((1,), (1,)), ((), ())), preferred_element_type=F32)


def tn(a, b):
    return lax.dot_general(a, b, (((0,), (0,)), ((), ())), preferred_element_type=F32)


def iota(shape, dim):
    return lax.broadcasted_iota(jnp.int32, shape, dim)


def listed(stages, chunks, row_bytes):
    now, free, done = 0.0, {}, [0] * len(stages)
    arrival = {(0, k): 0.0 for k in range(chunks)}
    for _ in range(len(stages) * chunks):
        open_now = [
            (number, k) for number, k in enumerate(done) if k < chunks and (number, k) in arrival
        ]
        ready = [item for item in open_now if arrival[item] <= now]
        number, k = max(ready) if ready else min(open_now, key=lambda item: arrival[item])
        stage, work, sends = stages[number]
        stage(k)
        done[number] += 1
        now = max(now, arrival[number, k]) + STEP_US + work / chunks
        arrived = now
        for link, rows in sends:
            free[link] = max(now, free.get(link, 0.0)) + rows * row_bytes / LINK_RATE[link]
            arrived = max(arrived, free[link] + HOP_US)
        arrival[number + 1, k] = arrived


def kernel(
    experts, cap, fold, cp, entering, routes, gates, saved_hbm, w_in_hbm, w_out_hbm, out,
    w_in, w_out, saved, silu_g, slope_u, acc, act, weight, place, merge,
    gbuf, rbuf, agbuf, pbuf, sibbuf, qbuf, rsbuf, ubuf, vbuf, xbuf,
    load_sem, cross_s, cross_r, ag_s, ag_r, fw_s, fw_r, sib_s, sib_r,
    rs_s, rs_r, ret_s, ret_r, x_s, x_r,
):
    sec = lax.axis_index("section")
    me = lax.axis_index("expert")
    e, j = lax.div(me, SHARDS), lax.rem(me, SHARDS)
    q, c = lax.div(j, 2), lax.rem(j, 2)
    parity = lax.rem(sec, 2)
    tok, width = entering.shape
    dk = width // CHUNKS
    rows = experts * cap
    half = CHIPS * rows
    hdev = w_out.shape[0]

    def at_expert(o):
        return (sec, lax.rem(e + o, experts) * SHARDS + j)

    def at_chip(o):
        return (sec, e * SHARDS + lax.rem(q + o, CHIPS) * 2 + c)

    y = lax.rem(q, 2)
    over = {1: 1 + 2 * y, 2: 2, 3: 3 - 2 * y}
    sibling = (sec, me + 1 - 2 * c)
    partner = (sec + 1 - 2 * parity, me)

    loads = [
        pltpu.make_async_copy(src, dst, load_sem.at[i])
        for i, (src, dst) in enumerate(
            ((saved_hbm, saved), (w_in_hbm, w_in), (w_out_hbm, w_out))
        )
    ]
    for load in loads:
        load.start()

    barrier = pltpu.get_barrier_semaphore()
    greeted = (
        [at_expert(o) for o in range(1, experts)]
        + [at_chip(o) for o in range(1, CHIPS)]
        + [sibling, partner]
    )
    for device in greeted:
        pl.semaphore_signal(barrier, inc=1, device_id=device, device_id_type=MESH)

    earlier = (iota((tok, tok), 1) < iota((tok, tok), 0)).astype(BF16)
    same = iota((tok, tok), 1) == iota((tok, tok), 0)

    def column(row):
        return jnp.sum(jnp.where(same, row.astype(F32), 0.0), axis=1, keepdims=True)

    for tick in range(2):
        route = column(routes[tick]).astype(jnp.int32)
        weight[tick] = column(gates[tick])
        onehot = (route == iota((tok, 128), 1)).astype(F32)
        before = nn(earlier, onehot.astype(BF16))
        slot = jnp.sum(before * onehot, axis=1, keepdims=True).astype(jnp.int32)
        for h in range(fold):
            target = route * cp + h * cap + slot
            spots = target == iota((tok, experts * cp), 1)
            place[tick, h] = spots.astype(F32).astype(BF16)
    r = iota((rows, experts * cp), 0)
    for h in range(fold):
        spots = r // cap * cp + h * cap + r % cap == iota((rows, experts * cp), 1)
        merge[h] = spots.astype(F32).astype(BF16)

    pl.semaphore_wait(barrier, len(greeted))

    def copy(src, dst, send, recv, device):
        return pltpu.make_async_remote_copy(
            src_ref=src, dst_ref=dst, send_sem=send, recv_sem=recv,
            device_id=device, device_id_type=MESH,
        )

    sent = []

    def send(src, dst, send_sem, recv_sem, device):
        one = copy(src, dst, send_sem, recv_sem, device)
        one.start()
        sent.append(one)

    def arrive(dst, send_sem, recv_sem, device):
        copy(dst, dst, send_sem, recv_sem, device).wait_recv()

    def ds(index, size):
        return pl.ds(pl.multiple_of(index * size, size), size)

    def cols(k):
        return slice(k * dk, (k + 1) * dk)

    def tokens(t, k):
        return entering[:, cols(k)] if t == 0 else xbuf[k]

    def part_of(h):
        return slice(h * dk // fold, (h + 1) * dk // fold)

    def folded(tables, data):
        total = tn(tables[0], data[:, part_of(0)])
        for h in range(1, fold):
            total = total + tn(tables[h], data[:, part_of(h)])
        return total.astype(BF16)

    def prepare_saved():
        loads[0].wait()
        total = SHARDS * rows
        r = iota((total, total), 0)
        block, inner = r // rows, r % rows
        source_j = block % CHIPS * 2 + block // CHIPS
        column = (inner // cap * SHARDS + source_j) * cap + inner % cap
        perm = (column == iota((total, total), 1)).astype(F32).astype(BF16)
        ordered = nn(perm, saved[...])
        gate_vals, up_vals = ordered[:, :hdev], ordered[:, hdev:]
        silu_g[...] = jax.nn.silu(gate_vals)
        slope_u[...] = up_vals * silu_slope(gate_vals)

    def dispatch(t, forward):
        def spread(k):
            if t == 1:
                arrive(xbuf.at[k], x_s.at[k], x_r.at[k], partner)
            gbuf[t, k] = folded(place[t], tokens(t, k))
            for o in range(1, experts):
                send(
                    gbuf.at[t, k, ds(lax.rem(e + o, experts), cp)],
                    rbuf.at[t, k, ds(e, cp)],
                    cross_s.at[t, k, o], cross_r.at[t, k, o], at_expert(o),
                )
            rbuf[t, k, ds(e, cp)] = gbuf[t, k, ds(e, cp)]
            if t == 0 and k == 2:
                prepare_saved()

        def gather(k):
            for o in range(1, experts):
                arrive(
                    rbuf.at[t, k, ds(lax.rem(e + experts - o, experts), cp)],
                    cross_s.at[t, k, o], cross_r.at[t, k, o], at_expert(o),
                )
            mine = ds(c * CHIPS + q, rows)
            for h in range(fold):
                agbuf[t, k, mine, part_of(h)] = nn(merge[h], rbuf[t, k]).astype(BF16)
            for i in (1, 2) if k % 2 else (1, 2, 3):
                spread_to(k, i, mine)

        def spread_to(k, i, block, to=None):
            send(
                agbuf.at[t, k, block], agbuf.at[t, k, block],
                ag_s.at[t, k, i], ag_r.at[t, k, i], at_chip(over[to or i]),
            )

        def landed(k, i):
            block = ds(c * CHIPS + lax.rem(q + over[i], CHIPS), rows)
            arrive(agbuf.at[t, k, block], ag_s.at[t, k, i], ag_r.at[t, k, i], at_chip(over[i]))
            return block

        def pass_on(k):
            if k % 2:
                spread_to(k, 3, landed(k, 2), to=1)

        def forward_on(k):
            for i in (1, 3) if k % 2 else (1, 2, 3):
                landed(k, i)
            send(
                agbuf.at[t, k, ds(c, half)], agbuf.at[t, k, ds(c, half)],
                fw_s.at[t, k], fw_r.at[t, k], sibling,
            )

        def multiply(k):
            if t == 0 and k == 0:
                loads[1].wait()
                loads[2].wait()
            arrive(agbuf.at[t, k, ds(1 - c, half)], fw_s.at[t, k], fw_r.at[t, k], sibling)

            @pl.when(forward)
            def _():
                part = nn(agbuf[t, k], w_in[cols(k), :])
                acc[...] = part if k == 0 else acc[...] + part

            @pl.when(jnp.logical_not(forward))
            def _():
                part = nt(agbuf[t, k], w_out[:, cols(k)])
                acc[:, :hdev] = part if k == 0 else acc[:, :hdev] + part

            if k == CHUNKS - 1:
                activate(forward)

        return [
            (spread, 1.0, [("z", cp // fold), ("mid", 2 * cp // fold)]),
            (gather, 1.0, [("y", 3 * rows // 2), ("z", 3 * rows // 2)]),
            (pass_on, 0.0, [("y", rows // 2)]),
            (forward_on, 0.0, [("core", half)]),
            (multiply, 4.0, []),
        ]

    def activate(forward):
        @pl.when(forward)
        def _():
            hidden = jax.nn.silu(acc[:, :hdev]) * acc[:, hdev:]
            act[:, :hdev] = hidden.astype(BF16)

        @pl.when(jnp.logical_not(forward))
        def _():
            d_hidden = acc[:, :hdev]
            act[:, :hdev] = (d_hidden * slope_u[...]).astype(BF16)
            act[:, hdev:] = (d_hidden * silu_g[...]).astype(BF16)

    def give_back(t, forward):
        def part(k):
            @pl.when(forward)
            def _():
                pbuf[t, k] = nn(act[:, :hdev], w_out[:, cols(k)]).astype(BF16)

            @pl.when(jnp.logical_not(forward))
            def _():
                pbuf[t, k] = nt(act[...], w_in[cols(k), :]).astype(BF16)

            send(
                pbuf.at[t, k, ds(1 - c, half)], sibbuf.at[t, k],
                sib_s.at[t, k], sib_r.at[t, k], sibling,
            )

        def scatter(k):
            arrive(sibbuf.at[t, k], sib_s.at[t, k], sib_r.at[t, k], sibling)
            both = pbuf[t, k, ds(c, half)].astype(F32) + sibbuf[t, k].astype(F32)
            qbuf[t, k] = both.astype(BF16)
            for o in range(1, CHIPS):
                send(
                    qbuf.at[t, k, ds(lax.rem(q + o, CHIPS), rows)], rsbuf.at[t, k, o],
                    rs_s.at[t, k, o], rs_r.at[t, k, o], at_chip(o),
                )

        def return_on(k):
            total = qbuf[t, k, ds(q, rows)].astype(F32)
            for o in range(1, CHIPS):
                arrive(rsbuf.at[t, k, o], rs_s.at[t, k, o], rs_r.at[t, k, o], at_chip(o))
                total = total + rsbuf[t, k, o].astype(F32)
            ubuf[t, k] = folded(merge[...], total.astype(BF16))
            for o in range(1, experts):
                send(
                    ubuf.at[t, k, ds(lax.rem(e + o, experts), cp)],
                    vbuf.at[t, k, ds(e, cp)],
                    ret_s.at[t, k, o], ret_r.at[t, k, o], at_expert(o),
                )
            vbuf[t, k, ds(e, cp)] = ubuf[t, k, ds(e, cp)]

        def combine(k):
            for o in range(1, experts):
                arrive(
                    vbuf.at[t, k, ds(lax.rem(e + experts - o, experts), cp)],
                    ret_s.at[t, k, o], ret_r.at[t, k, o], at_expert(o),
                )
            picked = jnp.concatenate([nn(place[t, h], vbuf[t, k]) for h in range(fold)], axis=1)
            result = (tokens(t, k).astype(F32) + weight[t] * picked).astype(BF16)
            out[t, :, cols(k)] = result
            if t == 0:
                stage_x[k] = result
                send(stage_x.at[k], xbuf.at[k], x_s.at[k], x_r.at[k], partner)

        return [
            (part, 4.0, [("core", half)]),
            (scatter, 1.5, [("y", 2 * rows), ("z", 2 * rows)]),
            (return_on, 1.0, [("z", cp // fold), ("mid", 2 * cp // fold)]),
            (combine, 0.7, [("x", tok)]),
        ]

    stage_x, xbuf = xbuf.at[0], xbuf.at[1]
    first, second = parity == 0, parity == 1
    listed(dispatch(0, first), CHUNKS, 2 * dk)
    listed(give_back(0, first) + dispatch(1, second), CHUNKS, 2 * dk)
    listed(give_back(1, second), CHUNKS, 2 * dk)
    for one in sent:
        one.wait_send()


def shards(entering, saved, routes, gates, w_in, w_out):
    experts = lax.axis_size("expert") // SHARDS
    tok, width = entering.shape[1:]
    top = routes.shape[3]
    assert top == 1
    cap = min(tok, max(2, (3 * tok * top + 2 * experts - 1) // (2 * experts)))
    fold = 2 if cap % 16 and 2 * cap % 16 == 0 else 1
    cp = -(-fold * cap // 16) * 16
    rows = experts * cap
    total = SHARDS * rows
    half = CHIPS * rows
    hdev = w_out.shape[2]
    dk = width // CHUNKS
    steps = (2, CHUNKS)
    dma = pltpu.SemaphoreType.DMA
    vmem = pl.BlockSpec(memory_space=pltpu.VMEM)
    hbm = pl.BlockSpec(memory_space=pl.ANY)
    out = pl.pallas_call(
        functools.partial(kernel, experts, cap, fold, cp),
        out_shape=jax.ShapeDtypeStruct((2, tok, width), BF16),
        in_specs=[vmem] * 3 + [hbm] * 3,
        out_specs=vmem,
        scratch_shapes=[
            pltpu.VMEM(w_in.shape[2:], BF16),
            pltpu.VMEM(w_out.shape[2:], BF16),
            pltpu.VMEM((total, 2 * hdev), BF16),
            pltpu.VMEM((total, hdev), F32),
            pltpu.VMEM((total, hdev), F32),
            pltpu.VMEM((total, 2 * hdev), F32),
            pltpu.VMEM((total, 2 * hdev), BF16),
            pltpu.VMEM((2, tok, 1), F32),
            pltpu.VMEM((2, fold, tok, experts * cp), BF16),
            pltpu.VMEM((fold, rows, experts * cp), BF16),
            pltpu.VMEM(steps + (experts * cp, dk // fold), BF16),
            pltpu.VMEM(steps + (experts * cp, dk // fold), BF16),
            pltpu.VMEM(steps + (total, dk), BF16),
            pltpu.VMEM(steps + (total, dk), BF16),
            pltpu.VMEM(steps + (half, dk), BF16),
            pltpu.VMEM(steps + (half, dk), BF16),
            pltpu.VMEM(steps + (CHIPS, rows, dk), BF16),
            pltpu.VMEM(steps + (experts * cp, dk // fold), BF16),
            pltpu.VMEM(steps + (experts * cp, dk // fold), BF16),
            pltpu.VMEM(steps + (tok, dk), BF16),
            dma((3,)),
            dma(steps + (experts,)), dma(steps + (experts,)),
            dma(steps + (CHIPS,)), dma(steps + (CHIPS,)),
            dma(steps), dma(steps),
            dma(steps), dma(steps),
            dma(steps + (CHIPS,)), dma(steps + (CHIPS,)),
            dma(steps + (experts,)), dma(steps + (experts,)),
            dma((CHUNKS,)), dma((CHUNKS,)),
        ],
        compiler_params=pltpu.CompilerParams(
            collective_id=0, has_side_effects=True, vmem_limit_bytes=56 * 1024 * 1024
        ),
    )(
        entering[0], routes.reshape(2, 1, tok), gates.reshape(2, 1, tok),
        saved[0, 0], w_in[0, 0], w_out[0, 0],
    )
    return out[:, None]


def solution(mesh):
    return jax.shard_map(
        shards,
        mesh=mesh,
        in_specs=(
            P("section", "expert", None),
            P("section", "expert", None, None),
            P(None, "section", "expert", None),
            P(None, "section", "expert", None),
            P("section", "expert", None, None),
            P("section", "expert", None, None),
        ),
        out_specs=P(None, "section", "expert", None),
        check_vma=False,
    )
```

```python
import functools

import jax
import jax.numpy as jnp
from jax import lax
from jax.experimental import pallas as pl
from jax.experimental.pallas import tpu as pltpu
from jax.sharding import PartitionSpec as P

SHARDS = 8
CHIPS = 4
CHUNKS = 7
HOP_US = 1.5
STEP_US = 0.3
LINK_RATE = {"y": 5e4, "z": 5e4, "mid": 5e4, "x": 5e4, "core": 6e5}
MESH = pl.DeviceIdType.MESH
F32 = jnp.float32
BF16 = jnp.bfloat16


def silu_slope(gate_vals):
    sigmoid_vals = jax.nn.sigmoid(gate_vals)
    return sigmoid_vals * (1.0 + gate_vals * (1.0 - sigmoid_vals))


def nn(a, b):
    return jnp.dot(a, b, preferred_element_type=F32)


def nt(a, b):
    return lax.dot_general(a, b, (((1,), (1,)), ((), ())), preferred_element_type=F32)


def tn(a, b):
    return lax.dot_general(a, b, (((0,), (0,)), ((), ())), preferred_element_type=F32)


def iota(shape, dim):
    return lax.broadcasted_iota(jnp.int32, shape, dim)


def listed(stages, chunks, row_bytes):
    now, free, done = 0.0, {}, [0] * len(stages)
    arrival = {(0, k): 0.0 for k in range(chunks)}
    for _ in range(len(stages) * chunks):
        open_now = [
            (number, k) for number, k in enumerate(done) if k < chunks and (number, k) in arrival
        ]
        ready = [item for item in open_now if arrival[item] <= now]
        number, k = max(ready) if ready else min(open_now, key=lambda item: arrival[item])
        stage, work, sends = stages[number]
        stage(k)
        done[number] += 1
        now = max(now, arrival[number, k]) + STEP_US + work / chunks
        arrived = now
        for link, rows in sends:
            free[link] = max(now, free.get(link, 0.0)) + rows * row_bytes / LINK_RATE[link]
            arrived = max(arrived, free[link] + HOP_US)
        arrival[number + 1, k] = arrived


def kernel(
    experts, cap, fold, cp, entering, routes, gates, saved_hbm, w_in_hbm, w_out_hbm, out,
    w_in, w_out, saved, silu_g, slope_u, acc, act, weight, place, merge,
    gbuf, rbuf, agbuf, pbuf, sibbuf, qbuf, rsbuf, ubuf, vbuf, xbuf,
    load_sem, cross_s, cross_r, ag_s, ag_r, fw_s, fw_r, sib_s, sib_r,
    rs_s, rs_r, ret_s, ret_r, x_s, x_r,
):
    sec = lax.axis_index("section")
    me = lax.axis_index("expert")
    e, j = lax.div(me, SHARDS), lax.rem(me, SHARDS)
    q, c = lax.div(j, 2), lax.rem(j, 2)
    parity = lax.rem(sec, 2)
    tok, width = entering.shape
    dk = width // CHUNKS
    rows = experts * cap
    half = CHIPS * rows
    hdev = w_out.shape[0]

    def at_expert(o):
        return (sec, lax.rem(e + o, experts) * SHARDS + j)

    def at_chip(o):
        return (sec, e * SHARDS + lax.rem(q + o, CHIPS) * 2 + c)

    y = lax.rem(q, 2)
    over = {1: 1 + 2 * y, 2: 2, 3: 3 - 2 * y}
    sibling = (sec, me + 1 - 2 * c)
    partner = (sec + 1 - 2 * parity, me)

    loads = [
        pltpu.make_async_copy(src, dst, load_sem.at[i])
        for i, (src, dst) in enumerate(
            ((saved_hbm, saved), (w_in_hbm, w_in), (w_out_hbm, w_out))
        )
    ]
    for load in loads:
        load.start()

    barrier = pltpu.get_barrier_semaphore()
    greeted = (
        [at_expert(o) for o in range(1, experts)]
        + [at_chip(o) for o in range(1, CHIPS)]
        + [sibling, partner]
    )
    for device in greeted:
        pl.semaphore_signal(barrier, inc=1, device_id=device, device_id_type=MESH)

    earlier = (iota((tok, tok), 1) < iota((tok, tok), 0)).astype(BF16)
    same = iota((tok, tok), 1) == iota((tok, tok), 0)

    def column(row):
        return jnp.sum(jnp.where(same, row.astype(F32), 0.0), axis=1, keepdims=True)

    for tick in range(2):
        route = column(routes[tick]).astype(jnp.int32)
        weight[tick] = column(gates[tick])
        onehot = (route == iota((tok, 128), 1)).astype(F32)
        before = nn(earlier, onehot.astype(BF16))
        slot = jnp.sum(before * onehot, axis=1, keepdims=True).astype(jnp.int32)
        for h in range(fold):
            target = route * cp + h * cap + slot
            spots = target == iota((tok, experts * cp), 1)
            place[tick, h] = spots.astype(F32).astype(BF16)
    r = iota((rows, experts * cp), 0)
    for h in range(fold):
        spots = r // cap * cp + h * cap + r % cap == iota((rows, experts * cp), 1)
        merge[h] = spots.astype(F32).astype(BF16)

    def copy(src, dst, send, recv, device):
        return pltpu.make_async_remote_copy(
            src_ref=src, dst_ref=dst, send_sem=send, recv_sem=recv,
            device_id=device, device_id_type=MESH,
        )

    sent = []

    def send(src, dst, send_sem, recv_sem, device):
        one = copy(src, dst, send_sem, recv_sem, device)
        one.start()
        sent.append(one)

    def arrive(dst, send_sem, recv_sem, device):
        copy(dst, dst, send_sem, recv_sem, device).wait_recv()

    def ds(index, size):
        return pl.ds(pl.multiple_of(index * size, size), size)

    def cols(k):
        return slice(k * dk, (k + 1) * dk)

    def tokens(t, k):
        return entering[:, cols(k)] if t == 0 else xbuf[k]

    def part_of(h):
        return slice(h * dk // fold, (h + 1) * dk // fold)

    def folded(tables, data):
        total = tn(tables[0], data[:, part_of(0)])
        for h in range(1, fold):
            total = total + tn(tables[h], data[:, part_of(h)])
        return total.astype(BF16)

    def prepare_saved():
        loads[0].wait()
        total = SHARDS * rows
        r = iota((total, total), 0)
        block, inner = r // rows, r % rows
        source_j = block % CHIPS * 2 + block // CHIPS
        column = (inner // cap * SHARDS + source_j) * cap + inner % cap
        perm = (column == iota((total, total), 1)).astype(F32).astype(BF16)
        ordered = nn(perm, saved[...])
        gate_vals, up_vals = ordered[:, :hdev], ordered[:, hdev:]
        silu_g[...] = jax.nn.silu(gate_vals)
        slope_u[...] = up_vals * silu_slope(gate_vals)

    def dispatch(t, forward):
        def spread(k):
            if t == 1:
                arrive(xbuf.at[k], x_s.at[k], x_r.at[k], partner)
            gbuf[t, k] = folded(place[t], tokens(t, k))
            for o in range(1, experts):
                send(
                    gbuf.at[t, k, ds(lax.rem(e + o, experts), cp)],
                    rbuf.at[t, k, ds(e, cp)],
                    cross_s.at[t, k, o], cross_r.at[t, k, o], at_expert(o),
                )
            rbuf[t, k, ds(e, cp)] = gbuf[t, k, ds(e, cp)]

        def gather(k):
            for o in range(1, experts):
                arrive(
                    rbuf.at[t, k, ds(lax.rem(e + experts - o, experts), cp)],
                    cross_s.at[t, k, o], cross_r.at[t, k, o], at_expert(o),
                )
            mine = ds(c * CHIPS + q, rows)
            for h in range(fold):
                agbuf[t, k, mine, part_of(h)] = nn(merge[h], rbuf[t, k]).astype(BF16)
            for i in (1, 2) if k % 2 else (1, 2, 3):
                spread_to(k, i, mine)

        def spread_to(k, i, block, to=None):
            send(
                agbuf.at[t, k, block], agbuf.at[t, k, block],
                ag_s.at[t, k, i], ag_r.at[t, k, i], at_chip(over[to or i]),
            )

        def landed(k, i):
            block = ds(c * CHIPS + lax.rem(q + over[i], CHIPS), rows)
            arrive(agbuf.at[t, k, block], ag_s.at[t, k, i], ag_r.at[t, k, i], at_chip(over[i]))
            return block

        def pass_on(k):
            if k % 2:
                spread_to(k, 3, landed(k, 2), to=1)

        def forward_on(k):
            for i in (1, 3) if k % 2 else (1, 2, 3):
                landed(k, i)
            send(
                agbuf.at[t, k, ds(c, half)], agbuf.at[t, k, ds(c, half)],
                fw_s.at[t, k], fw_r.at[t, k], sibling,
            )

        def multiply(k):
            if t == 0 and k == 0:
                loads[1].wait()
                loads[2].wait()
            arrive(agbuf.at[t, k, ds(1 - c, half)], fw_s.at[t, k], fw_r.at[t, k], sibling)

            @pl.when(forward)
            def _():
                part = nn(agbuf[t, k], w_in[cols(k), :])
                acc[...] = part if k == 0 else acc[...] + part

            @pl.when(jnp.logical_not(forward))
            def _():
                part = nt(agbuf[t, k], w_out[:, cols(k)])
                acc[:, :hdev] = part if k == 0 else acc[:, :hdev] + part

            if k == CHUNKS - 1:
                activate(forward)

        return [
            (spread, 1.0, [("z", cp // fold), ("mid", 2 * cp // fold)]),
            (gather, 1.0, [("y", 3 * rows // 2), ("z", 3 * rows // 2)]),
            (pass_on, 0.0, [("y", rows // 2)]),
            (forward_on, 0.0, [("core", half)]),
            (multiply, 4.0, []),
        ]

    def activate(forward):
        @pl.when(forward)
        def _():
            hidden = jax.nn.silu(acc[:, :hdev]) * acc[:, hdev:]
            act[:, :hdev] = hidden.astype(BF16)

        @pl.when(jnp.logical_not(forward))
        def _():
            d_hidden = acc[:, :hdev]
            act[:, :hdev] = (d_hidden * slope_u[...]).astype(BF16)
            act[:, hdev:] = (d_hidden * silu_g[...]).astype(BF16)

    def give_back(t, forward):
        def part(k):
            @pl.when(forward)
            def _():
                pbuf[t, k] = nn(act[:, :hdev], w_out[:, cols(k)]).astype(BF16)

            @pl.when(jnp.logical_not(forward))
            def _():
                pbuf[t, k] = nt(act[...], w_in[cols(k), :]).astype(BF16)

            send(
                pbuf.at[t, k, ds(1 - c, half)], sibbuf.at[t, k],
                sib_s.at[t, k], sib_r.at[t, k], sibling,
            )

        def scatter(k):
            arrive(sibbuf.at[t, k], sib_s.at[t, k], sib_r.at[t, k], sibling)
            both = pbuf[t, k, ds(c, half)].astype(F32) + sibbuf[t, k].astype(F32)
            qbuf[t, k] = both.astype(BF16)
            for o in range(1, CHIPS):
                send(
                    qbuf.at[t, k, ds(lax.rem(q + o, CHIPS), rows)], rsbuf.at[t, k, o],
                    rs_s.at[t, k, o], rs_r.at[t, k, o], at_chip(o),
                )

        def return_on(k):
            total = qbuf[t, k, ds(q, rows)].astype(F32)
            for o in range(1, CHIPS):
                arrive(rsbuf.at[t, k, o], rs_s.at[t, k, o], rs_r.at[t, k, o], at_chip(o))
                total = total + rsbuf[t, k, o].astype(F32)
            ubuf[t, k] = folded(merge[...], total.astype(BF16))
            for o in range(1, experts):
                send(
                    ubuf.at[t, k, ds(lax.rem(e + o, experts), cp)],
                    vbuf.at[t, k, ds(e, cp)],
                    ret_s.at[t, k, o], ret_r.at[t, k, o], at_expert(o),
                )
            vbuf[t, k, ds(e, cp)] = ubuf[t, k, ds(e, cp)]

        def combine(k):
            for o in range(1, experts):
                arrive(
                    vbuf.at[t, k, ds(lax.rem(e + experts - o, experts), cp)],
                    ret_s.at[t, k, o], ret_r.at[t, k, o], at_expert(o),
                )
            picked = jnp.concatenate([nn(place[t, h], vbuf[t, k]) for h in range(fold)], axis=1)
            result = (tokens(t, k).astype(F32) + weight[t] * picked).astype(BF16)
            out[t, :, cols(k)] = result
            if t == 0:
                stage_x[k] = result
                send(stage_x.at[k], xbuf.at[k], x_s.at[k], x_r.at[k], partner)

        return [
            (part, 4.0, [("core", half)]),
            (scatter, 1.5, [("y", 2 * rows), ("z", 2 * rows)]),
            (return_on, 1.0, [("z", cp // fold), ("mid", 2 * cp // fold)]),
            (combine, 0.7, [("x", tok)]),
        ]

    prepare_saved()
    pl.semaphore_wait(barrier, len(greeted))
    stage_x, xbuf = xbuf.at[0], xbuf.at[1]
    first, second = parity == 0, parity == 1
    listed(dispatch(0, first), CHUNKS, 2 * dk)
    listed(give_back(0, first) + dispatch(1, second), CHUNKS, 2 * dk)
    listed(give_back(1, second), CHUNKS, 2 * dk)
    for one in sent:
        one.wait_send()


def shards(entering, saved, routes, gates, w_in, w_out):
    experts = lax.axis_size("expert") // SHARDS
    tok, width = entering.shape[1:]
    top = routes.shape[3]
    assert top == 1
    cap = min(tok, max(2, (3 * tok * top + 2 * experts - 1) // (2 * experts)))
    fold = 2 if cap % 16 and 2 * cap % 16 == 0 else 1
    cp = -(-fold * cap // 16) * 16
    rows = experts * cap
    total = SHARDS * rows
    half = CHIPS * rows
    hdev = w_out.shape[2]
    dk = width // CHUNKS
    steps = (2, CHUNKS)
    dma = pltpu.SemaphoreType.DMA
    vmem = pl.BlockSpec(memory_space=pltpu.VMEM)
    hbm = pl.BlockSpec(memory_space=pl.ANY)
    out = pl.pallas_call(
        functools.partial(kernel, experts, cap, fold, cp),
        out_shape=jax.ShapeDtypeStruct((2, tok, width), BF16),
        in_specs=[vmem] * 3 + [hbm] * 3,
        out_specs=vmem,
        scratch_shapes=[
            pltpu.VMEM(w_in.shape[2:], BF16),
            pltpu.VMEM(w_out.shape[2:], BF16),
            pltpu.VMEM((total, 2 * hdev), BF16),
            pltpu.VMEM((total, hdev), F32),
            pltpu.VMEM((total, hdev), F32),
            pltpu.VMEM((total, 2 * hdev), F32),
            pltpu.VMEM((total, 2 * hdev), BF16),
            pltpu.VMEM((2, tok, 1), F32),
            pltpu.VMEM((2, fold, tok, experts * cp), BF16),
            pltpu.VMEM((fold, rows, experts * cp), BF16),
            pltpu.VMEM(steps + (experts * cp, dk // fold), BF16),
            pltpu.VMEM(steps + (experts * cp, dk // fold), BF16),
            pltpu.VMEM(steps + (total, dk), BF16),
            pltpu.VMEM(steps + (total, dk), BF16),
            pltpu.VMEM(steps + (half, dk), BF16),
            pltpu.VMEM(steps + (half, dk), BF16),
            pltpu.VMEM(steps + (CHIPS, rows, dk), BF16),
            pltpu.VMEM(steps + (experts * cp, dk // fold), BF16),
            pltpu.VMEM(steps + (experts * cp, dk // fold), BF16),
            pltpu.VMEM(steps + (tok, dk), BF16),
            dma((3,)),
            dma(steps + (experts,)), dma(steps + (experts,)),
            dma(steps + (CHIPS,)), dma(steps + (CHIPS,)),
            dma(steps), dma(steps),
            dma(steps), dma(steps),
            dma(steps + (CHIPS,)), dma(steps + (CHIPS,)),
            dma(steps + (experts,)), dma(steps + (experts,)),
            dma((CHUNKS,)), dma((CHUNKS,)),
        ],
        compiler_params=pltpu.CompilerParams(
            collective_id=0, has_side_effects=True, vmem_limit_bytes=56 * 1024 * 1024
        ),
    )(
        entering[0], routes.reshape(2, 1, tok), gates.reshape(2, 1, tok),
        saved[0, 0], w_in[0, 0], w_out[0, 0],
    )
    return out[:, None]


def solution(mesh):
    return jax.shard_map(
        shards,
        mesh=mesh,
        in_specs=(
            P("section", "expert", None),
            P("section", "expert", None, None),
            P(None, "section", "expert", None),
            P(None, "section", "expert", None),
            P("section", "expert", None, None),
            P("section", "expert", None, None),
        ),
        out_specs=P(None, "section", "expert", None),
        check_vma=False,
    )
```
